512 devices in a mesh: wide: 64 (over z, y), narrow: 8 (over x, core).
Axes of the slice: x: 4, y: 4, z: 16, core: 2. Of those that a mesh axis runs over, the one named last changes fastest.
Arguments:
- density: bfloat16 [32, 262144], P(None, ('wide', 'narrow')), may hold values from -6 to 6
- panels: float32 [7, 262144], P(None, ('wide', 'narrow')), as said below
- near_mask: int32 [2048, 8], P(('wide', 'narrow')), may hold values from 0 to 1, as said below
- source_basis: bfloat16 [64, 262144], P(None, ('wide', 'narrow')), may hold values from -0.5 to 0.5
- leaf_transfer: bfloat16 [2048, 64, 64], P(('wide', 'narrow')), may hold values from -0.375 to 0.375
- cluster_coupling: bfloat16 [512, 512, 64], P(('wide', 'narrow')), may hold values from -0.25 to 0.25
- out_leaf: int32 [32768], P(('wide', 'narrow')), may hold values from 0 to 3
- out_wide: int32 [32768, 1], P(('wide', 'narrow')), may hold values from 0 to 63; in each aligned block of 64 rows (0 to 63, 64 to 127, ...) at most 2 rows name the same one
- out_target: int32 [32768], P(('wide', 'narrow')), may hold values from 0 to 3
- coupling: bfloat16 [32768, 64, 64], P(('wide', 'narrow')), may hold values from -0.1875 to 0.1875
- target_basis: bfloat16 [64, 262144], P(None, ('wide', 'narrow')), may hold values from -0.75 to 0.75
Outputs:
- first_pass: bfloat16 [32, 262144], P(None, ('wide', 'narrow'))
- second_pass: bfloat16 [32, 262144], P(None, ('wide', 'narrow'))
The draws below stay inside these ranges and needn't reach their ends.
Inputs may be any that keep to these rules, and one draw needn't show every extreme that they name: `panels`: rows 0 to 2 hold panel positions, rows 3 to 5 unit normals, row 6 panel areas between 0.05 and 0.4. near_mask[g, c] is 0 wherever c % 4 and g % 4 differ by more than 1, and 1 where c = g % 4. `out_wide`: among the 64 coupling blocks of one device no wide index is named more than 2 times, and some wide index is named exactly 2 times.
All inputs are finite; a program needn't handle non-finite values.
Results may differ from the reference program's by a relative error of at most 0.012.
Values may be sent and summed in bfloat16 or wider, within the bound.
No kernel may reach another device: no remote copies, remote signals or barrier semaphores. Data moves between devices by JAX's collectives and lax.ppermute only.
A program may use at most 64 MiB of HBM per device.

```python
import math
import jax
import jax.numpy as jnp
import numpy as np
from jax import lax

LEAF_SIZE = 128
RANK = 64
RIGHT_SIDES = 32
PARTNERS = 16
LEAF_DEV = 4
OUT_DEV = 64
CAP = 2
LEAVES = 2048
PANELS = 262144
OUTS = 32768
N_WIDE = 64
N_NARROW = 8
DEVICES = 512


def draw_panels(key, part):
    key = jax.random.fold_in(key, 11)
    key_jitter, key_azimuth, key_polar, key_areas = jax.random.split(key, 4)
    leaf_id = jnp.arange(PANELS, dtype=jnp.int32) // LEAF_SIZE
    device_id = leaf_id // LEAF_DEV
    in_device = leaf_id % LEAF_DEV
    centre_x = (device_id // 2).astype(jnp.float32) * 3.0
    centre_y = in_device.astype(jnp.float32)
    centre_z = (device_id % 2).astype(jnp.float32)
    jitter = jax.random.uniform(key_jitter, (3, PANELS), jnp.float32, -0.5, 0.5)
    azimuth = jax.random.uniform(key_azimuth, (PANELS,), jnp.float32, 0.0, 2.0 * math.pi)
    polar_cos = jax.random.uniform(key_polar, (PANELS,), jnp.float32, -1.0, 1.0)
    polar_sin = jnp.sqrt(jnp.maximum(1.0 - polar_cos * polar_cos, 0.0))
    uniform_area = jax.random.uniform(key_areas, (PANELS,), jnp.float32, 0.0, 1.0)
    areas = 0.1 + 0.2 * uniform_area
    rows = [centre_x + jitter[0], centre_y + jitter[1], centre_z + jitter[2], polar_sin * jnp.cos(azimuth), polar_sin * jnp.sin(azimuth), polar_cos, areas]
    return jnp.stack(rows, axis=0).astype(jnp.float32)


def draw_near_mask(key, part):
    key = jax.random.fold_in(key, 23)
    row_slot = jnp.arange(LEAVES, dtype=jnp.int32) % LEAF_DEV
    column_id = jnp.arange(2 * LEAF_DEV, dtype=jnp.int32)
    column_slot = column_id % LEAF_DEV
    distance = jnp.abs(row_slot[:, None] - column_slot[None, :])
    itself = column_id[None, :] == row_slot[:, None]
    kept = jax.random.randint(key, (LEAVES, 2 * LEAF_DEV), 0, 4) > 0
    near = jnp.where(itself, True, jnp.logical_and(distance <= 1, kept))
    return near.astype(jnp.int32)


def set_ends(result, stream_key, smallest, top_value):
    place = [jax.random.randint(jax.random.fold_in(stream_key, axis), (), 0, length) for axis, length in enumerate(result.shape)]
    longest = result.shape.index(max(result.shape))
    neighbour = place[:longest] + [(place[longest] + 1) % result.shape[longest]] + place[longest + 1:]
    return result.at[tuple(place)].set(smallest).at[tuple(neighbour)].set(top_value)


def steps_of(key, dims, cuts, low, high):
    loudness = 1.0
    for dim, parts in cuts:
        draws = jax.random.uniform(jax.random.fold_in(jax.random.fold_in(key, 6), dim), (parts,), jnp.float32, low / len(cuts), high / len(cuts))
        loudness = loudness * jnp.repeat(jnp.exp(draws), dims[dim] // parts).reshape((-1,) + (1,) * (len(dims) - 1 - dim))
    return loudness


def deal_out(key, own, number, rows, count, top, limit, lean):
    sequence = jax.random.permutation(key, count)
    heavy_load, common = portions_of(count, rows * top, limit, lean, True), portions_of(count, rows * top, limit, lean, False)
    places = jnp.arange(count)

    def named(lengths, turn):
        used = int((lengths > 0).sum())
        fixed = max(1, used // 4)
        shifted = fixed + (places - fixed + turn * (used - fixed)) % max(1, count - fixed)
        return jnp.zeros((count,), jnp.int32).at[sequence[jnp.where(places < fixed, places, shifted)]].set(jnp.asarray(lengths, jnp.int32))

    lengths = jnp.where(number % 4 == 0, named(heavy_load, number // 4), named(common, number - number // 4 - 1))
    mixed = jax.random.permutation(jax.random.fold_in(own, 3), count)
    source_of, sink = mixed[0:count // 2 * 2:2], mixed[1:count // 2 * 2:2]
    room = jnp.minimum(lengths[source_of] - 1, limit - lengths[sink]) // 2
    room = jnp.where((source_of == sequence[0]) | (sink == sequence[0]) | (lengths[sink] == 0), 0, jnp.maximum(room, 0))
    shifted = jax.random.randint(jax.random.fold_in(own, 4), (count // 2,), 0, 1 << 20) % (room + 1)
    lengths = lengths.at[source_of].add(-shifted).at[sink].add(shifted)
    items = jnp.searchsorted(jnp.cumsum(lengths), jnp.arange(rows * top), side="right").astype(jnp.int32)
    listing = items.reshape(top, rows).T
    listing = listing[jax.random.permutation(jax.random.fold_in(own, 1), rows)]
    turn = jax.random.randint(jax.random.fold_in(own, 2), (rows, 1), 0, top)
    return jnp.take_along_axis(listing, (jnp.arange(top)[None, :] + turn) % top, axis=1)


def portions_of(count, total, bound, slope, full):
    loads = [(1 << 20) // math.isqrt(standing ** slope) + 1 for standing in range(1, count + 1)]
    largest = bound if full else min(bound, max(-(-total // count), total * loads[0] // sum(loads)))
    least = 1 if total - largest >= count - 1 else 0
    holding, rest = [largest] + [least] * (count - 1), total - largest - least * (count - 1)
    while rest > 0:
        free = [i for i in range(1, count) if holding[i] < largest] or [i for i in range(1, count) if holding[i] < bound]
        mass, left = sum([loads[i] for i in free]), rest
        for i in free:
            addition = min(bound - holding[i], max(1, left * loads[i] // mass), rest)
            holding[i] = holding[i] + addition
            rest = rest - addition
    return np.array(holding)


def normal_values(rng, extent, width, most, shards=(), kind=jnp.bfloat16):
    values = jax.random.normal(rng, extent, jnp.float32) * width
    if len(shards) > 0:
        values = steps_of(rng, extent, shards, -0.22, 0.18) * values
    return jnp.clip(values, min=-most, max=most).astype(kind)


def setup_inputs(seed: int = 0) -> dict:
    streams_of = jax.random.split(jax.random.key(seed), 12)
    density = normal_values(streams_of[0], (RIGHT_SIDES, PANELS), 1.0, 6.0, ((1, 512),))
    panels = draw_panels(jax.random.fold_in(streams_of[11], 71), 0)
    near_mask = draw_near_mask(jax.random.fold_in(streams_of[11], 71), 0)
    source_basis = normal_values(streams_of[3], (RANK, PANELS), LEAF_SIZE ** -0.5, 0.5, ((1, 512),))
    leaf_transfer = normal_values(streams_of[4], (LEAVES, RANK, RANK), (RANK * LEAF_DEV) ** -0.5, 0.375, ((0, 512),))
    cluster_coupling = normal_values(streams_of[5], (N_WIDE * N_NARROW, N_NARROW * RANK, RANK), (N_NARROW * RANK) ** -0.5, 0.25, ((0, 512),))
    out_leaf = set_ends(jax.random.randint(streams_of[6], (OUTS,), 0, LEAF_DEV), jax.random.fold_in(streams_of[6], 1), 0, LEAF_DEV - 1).astype(jnp.int32)
    out_wide_keys = jax.random.split(jax.random.fold_in(streams_of[7], 1), OUTS // OUT_DEV)
    out_wide_turns = jax.random.permutation(jax.random.fold_in(streams_of[7], 3), OUTS // OUT_DEV)
    out_wide = jax.vmap(lambda own, number: deal_out(jax.random.fold_in(streams_of[7], 2), own, number, OUT_DEV, N_WIDE, 1, CAP, 2))(out_wide_keys, out_wide_turns).reshape((OUTS, 1))
    out_target = set_ends(jax.random.randint(streams_of[8], (OUTS,), 0, LEAF_DEV), jax.random.fold_in(streams_of[8], 1), 0, LEAF_DEV - 1).astype(jnp.int32)
    coupling = normal_values(streams_of[9], (OUTS, RANK, RANK), (RANK * PARTNERS) ** -0.5, 0.1875, ((0, 512),))
    target_basis = normal_values(streams_of[10], (RANK, PANELS), RANK ** -0.5, 0.75, ((1, 512),))
    return dict(density=density, panels=panels, near_mask=near_mask, source_basis=source_basis, leaf_transfer=leaf_transfer, cluster_coupling=cluster_coupling, out_leaf=out_leaf, out_wide=out_wide, out_target=out_target, coupling=coupling, target_basis=target_basis)


SMOOTHING = 0.0625

def kernel_block(target_pos, source_geom):
    offsets = target_pos[:, :, None] - source_geom[0:3, None, :]
    squared = lax.optimization_barrier(jnp.sum(offsets * offsets, axis=0)) + SMOOTHING
    normal_dot = lax.optimization_barrier(jnp.sum(source_geom[3:6, None, :] * offsets, axis=0))
    return source_geom[6][None, :] * normal_dot / (4.0 * math.pi * squared * jnp.sqrt(squared))

def device_nearby(own_geom, source_geom, source_density, near_rows):
    target_pos = jnp.transpose(own_geom[0:3].reshape(3, LEAF_DEV, LEAF_SIZE), (1, 0, 2))
    weights = jnp.repeat(near_rows.astype(jnp.bfloat16), LEAF_SIZE, axis=1)

    def leaf_near(position, weight_row):
        kernel = kernel_block(position, source_geom).astype(jnp.bfloat16) * weight_row[None, :]
        return jnp.dot(source_density.astype(jnp.float32), kernel.astype(jnp.float32).T)
    blocks = jax.vmap(leaf_near)(target_pos, weights)
    return jnp.transpose(blocks, (1, 0, 2)).reshape(RIGHT_SIDES, LEAF_DEV * LEAF_SIZE)

def reference(density, panels, near_mask, source_basis, leaf_transfer, cluster_coupling, out_leaf, out_wide, out_target, coupling, target_basis):
    span_len = LEAF_DEV * LEAF_SIZE
    transfer_f = leaf_transfer.reshape(DEVICES, LEAF_DEV, RANK, RANK).astype(jnp.float32)

    def apply_operator(values):
        coeffs = jnp.einsum('rls,kls->lrk', values.reshape(RIGHT_SIDES, LEAVES, LEAF_SIZE).astype(jnp.float32), source_basis.reshape(RANK, LEAVES, LEAF_SIZE).astype(jnp.float32)).astype(jnp.bfloat16)
        cluster = jnp.einsum('dlrk,dlkj->drj', coeffs.reshape(DEVICES, LEAF_DEV, RIGHT_SIDES, RANK).astype(jnp.float32), transfer_f).astype(jnp.bfloat16)
        grouped = cluster.reshape(N_WIDE, N_NARROW, RIGHT_SIDES, RANK).astype(jnp.float32)
        downward = jnp.einsum('wmrk,wnmkj->wnrj', grouped, cluster_coupling.reshape(N_WIDE, N_NARROW, N_NARROW, RANK, RANK).astype(jnp.float32))
        downward = downward.reshape(DEVICES, RIGHT_SIDES, RANK)

        def add_device(leaf_field, device_id):
            offset = device_id * OUT_DEV
            sources = lax.dynamic_slice_in_dim(out_leaf, offset, OUT_DEV) + device_id * LEAF_DEV
            wide_ids = lax.dynamic_slice_in_dim(out_wide[:, 0], offset, OUT_DEV)
            local_ids = lax.dynamic_slice_in_dim(out_target, offset, OUT_DEV)
            targets = ((wide_ids * N_NARROW + device_id % N_NARROW) * LEAF_DEV + local_ids).astype(jnp.int32)
            blocks = lax.dynamic_slice_in_dim(coupling, offset, OUT_DEV, 0).astype(jnp.float32)
            products = jnp.einsum('erk,ekj->erj', coeffs[sources.astype(jnp.int32)].astype(jnp.float32), blocks)
            return (leaf_field.at[targets].add(products), None)
        leaf_field, _ = lax.scan(add_device, jnp.zeros((LEAVES, RIGHT_SIDES, RANK), jnp.float32), jnp.arange(DEVICES, dtype=jnp.int32))
        spread = jnp.einsum('drk,dljk->dlrj', downward, transfer_f).reshape(LEAVES, RIGHT_SIDES, RANK)
        leaf_field = (leaf_field + spread).astype(jnp.bfloat16)
        far_part = jnp.einsum('lrk,kls->rls', leaf_field.astype(jnp.float32), target_basis.reshape(RANK, LEAVES, LEAF_SIZE).astype(jnp.float32)).reshape(RIGHT_SIDES, PANELS)

        def device_block(device_id):
            partner = jnp.bitwise_xor(device_id, 1)
            own_geom = lax.dynamic_slice_in_dim(panels, device_id * span_len, span_len, 1)
            other_geom = lax.dynamic_slice_in_dim(panels, partner * span_len, span_len, 1)
            own_values = lax.dynamic_slice_in_dim(values, device_id * span_len, span_len, 1)
            other_values = lax.dynamic_slice_in_dim(values, partner * span_len, span_len, 1)
            near_rows = lax.dynamic_slice_in_dim(near_mask, device_id * LEAF_DEV, LEAF_DEV, 0)
            return device_nearby(own_geom, jnp.concatenate([own_geom, other_geom], axis=1), jnp.concatenate([own_values, other_values], axis=1), near_rows)
        nearby = lax.map(device_block, jnp.arange(DEVICES, dtype=jnp.int32))
        near_part = jnp.transpose(nearby, (1, 0, 2)).reshape(RIGHT_SIDES, PANELS)
        return (0.5 * values.astype(jnp.float32) + near_part + far_part).astype(jnp.bfloat16)
    first_pass = apply_operator(density)
    second_pass = apply_operator(first_pass)
    return (first_pass, second_pass)
```

```python
import math

import jax
import jax.numpy as jnp
import numpy as np
from jax import lax
from jax.experimental import pallas as pl
from jax.experimental.pallas import tpu as pltpu
from jax.sharding import Mesh, PartitionSpec as P

LEAF_SIZE = 128
RANK = 64
RIGHT_SIDES = 32
LEAVES = 4
OUTS = 64
SMOOTHING = 0.0625
NZ, NY, NX, NC = 16, 4, 4, 2
NARROW = NX * NC
SLOTS = 2 * NZ
ROWS = 16
CHUNK = SLOTS * ROWS + SLOTS
EMPTY = 4
F32, BF16 = jnp.float32, jnp.bfloat16
NT = (((1,), (1,)), ((), ()))


def call(body, name, out_shape, in_spaces, scratch=()):
    return pl.pallas_call(
        body,
        out_shape=out_shape,
        in_specs=[pl.BlockSpec(memory_space=space) for space in in_spaces],
        out_specs=[pl.BlockSpec(memory_space=pltpu.VMEM)] * len(out_shape),
        scratch_shapes=list(scratch),
        compiler_params=pltpu.CompilerParams(vmem_limit_bytes=32 * 1024 * 1024),
        name=name,
    )


VM, SM = pltpu.VMEM, pltpu.SMEM


def dot(a, b, dims=None):
    if dims is None:
        return jnp.dot(a, b, preferred_element_type=F32)
    return lax.dot_general(a, b, dims, preferred_element_type=F32)


def pack(block):
    return jnp.concatenate([block[:ROWS], block[ROWS:]], axis=1)


def leaf_cols(leaf):
    return slice(leaf * LEAF_SIZE, (leaf + 1) * LEAF_SIZE)


def outgoing(value_ref, code_ref, basis_ref, transfer_ref, coupling_ref, send_ref, cluster_ref, coeff_ref, count_ref):
    cluster = jnp.zeros((RIGHT_SIDES, RANK), F32)
    for leaf in range(LEAVES):
        coeff = dot(value_ref[:, leaf_cols(leaf)], basis_ref[:, leaf_cols(leaf)], NT).astype(BF16)
        coeff_ref[leaf * RIGHT_SIDES : (leaf + 1) * RIGHT_SIDES, :] = coeff
        cluster += dot(coeff, transfer_ref[leaf])
    wide_cluster = jnp.concatenate([cluster, jnp.zeros_like(cluster)], axis=1).astype(BF16)
    for peer in range(NARROW):
        cluster_ref[peer] = wide_cluster
    for peer in range(NY):
        send_ref[peer] = jnp.concatenate(
            [jnp.zeros((SLOTS * ROWS, 128), BF16), jnp.full((SLOTS, 128), EMPTY, BF16)], axis=0
        )
    for wide in range(NZ * NY):
        count_ref[wide] = 0
    rows = lax.broadcasted_iota(jnp.int32, (SLOTS, 128), 0)
    for block in range(OUTS):
        code = code_ref[block]
        wide = code // 16
        target = (code // 4) % 4
        source = code % 4
        turn = count_ref[wide]
        count_ref[wide] = turn + 1
        peer = wide % NY
        slot = (wide // NY) * 2 + turn
        coeff = coeff_ref[pl.ds(pl.multiple_of(source * RIGHT_SIDES, RIGHT_SIDES), RIGHT_SIDES), :]
        product = dot(coeff, coupling_ref[block])
        send_ref[peer, pl.ds(pl.multiple_of(slot * ROWS, ROWS), ROWS), :] = pack(product).astype(BF16)
        ids = send_ref[peer, SLOTS * ROWS :, :]
        send_ref[peer, SLOTS * ROWS :, :] = jnp.where(rows == slot, target.astype(F32), ids.astype(F32)).astype(BF16)


def first_body(value_ref, code_ref, basis_ref, transfer_ref, coupling_ref, send_ref, cluster_ref, coeff_ref, count_ref):
    outgoing(value_ref, code_ref, basis_ref, transfer_ref, coupling_ref, send_ref, cluster_ref, coeff_ref, count_ref)


def merge_body(recv_ref, out_ref):
    ids = [recv_ref[src, SLOTS * ROWS :, :].astype(F32) for src in range(NY)]
    for z in range(NZ):
        total = [jnp.zeros((ROWS, 128), F32) for _ in range(LEAVES)]
        for src in range(NY):
            for turn in range(2):
                slot = z * 2 + turn
                block = recv_ref[src, slot * ROWS : (slot + 1) * ROWS, :].astype(F32)
                row = jnp.broadcast_to(ids[src][slot : slot + 1, :], (ROWS, 128))
                for leaf in range(LEAVES):
                    total[leaf] += jnp.where(row == leaf, block, 0.0)
        for leaf in range(LEAVES):
            out_ref[z, leaf * ROWS : (leaf + 1) * ROWS, :] = total[leaf].astype(BF16)


def kernel_body(own_ref, other_ref, mask_ref, kernel_ref):
    columns = jnp.transpose(
        jnp.concatenate([own_ref[0:3, :], jnp.zeros((5, LEAVES * LEAF_SIZE), F32)], axis=0)
    )
    for leaf in range(LEAVES):
        place = [columns[leaf_cols(leaf), axis : axis + 1] for axis in range(3)]
        for side, ref in enumerate((own_ref, other_ref)):
            for near in range(max(leaf - 1, 0), min(leaf + 2, LEAVES)):
                source = [ref[row : row + 1, leaf_cols(near)] for row in range(7)]
                offset = [place[axis] - source[axis] for axis in range(3)]
                squared = offset[0] * offset[0] + offset[1] * offset[1] + offset[2] * offset[2] + SMOOTHING
                along = offset[0] * source[3] + offset[1] * source[4] + offset[2] * source[5]
                inverse = lax.rsqrt(squared)
                kernel = (source[6] * (1.0 / (4.0 * math.pi))) * along * (inverse * inverse * inverse)
                keep = mask_ref[leaf, side * LEAVES + near] != 0
                first = side * LEAVES * LEAF_SIZE
                kernel_ref[leaf_cols(leaf), first + near * LEAF_SIZE : first + (near + 1) * LEAF_SIZE] = jnp.where(
                    keep, kernel, 0.0
                ).astype(BF16)


def near_body(value_ref, other_ref, kernel_ref, group_ref, rows_ref, transfer_ref, base_ref, spread_ref):
    for leaf in range(LEAVES):
        low, high = max(leaf - 1, 0) * LEAF_SIZE, min(leaf + 2, LEAVES) * LEAF_SIZE
        width = LEAVES * LEAF_SIZE
        near = dot(value_ref[:, low:high], kernel_ref[leaf_cols(leaf), low:high], NT)
        near += dot(other_ref[:, low:high], kernel_ref[leaf_cols(leaf), width + low : width + high], NT)
        base_ref[:, leaf_cols(leaf)] = near + 0.5 * value_ref[:, leaf_cols(leaf)].astype(F32)
    down = jnp.zeros((RIGHT_SIDES, RANK), F32)
    for peer in range(NARROW):
        down += dot(group_ref[peer, :, :RANK], rows_ref[0, peer * RANK : (peer + 1) * RANK, :])
    high = down.astype(BF16)
    low = (down - high.astype(F32)).astype(BF16)
    for leaf in range(LEAVES):
        spread = dot(high, transfer_ref[leaf], NT) + dot(low, transfer_ref[leaf], NT)
        spread_ref[leaf * ROWS : (leaf + 1) * ROWS, :] = pack(spread)


def finish(recv_ref, spread_ref, base_ref, target_ref, out_ref):
    field = spread_ref[...]
    for src in range(NZ):
        field += recv_ref[src].astype(F32)
    field = field.astype(BF16)
    lower = lax.broadcasted_iota(jnp.int32, (ROWS, 128), 1) < RANK
    for leaf in range(LEAVES):
        block = field[leaf * ROWS : (leaf + 1) * ROWS, :].astype(F32)
        tall = jnp.concatenate([jnp.where(lower, block, 0.0), jnp.where(lower, 0.0, block)], axis=0).astype(BF16)
        basis = target_ref[:, leaf_cols(leaf)]
        far = dot(tall, jnp.concatenate([basis, basis], axis=0))
        out_ref[:, leaf_cols(leaf)] = (base_ref[:, leaf_cols(leaf)] + far).astype(BF16)


def middle_body(
    recv_ref, spread_ref, base_ref, target_ref, code_ref, basis_ref, transfer_ref, coupling_ref,
    out_ref, send_ref, cluster_ref, coeff_ref, count_ref,
):
    finish(recv_ref, spread_ref, base_ref, target_ref, out_ref)
    outgoing(out_ref, code_ref, basis_ref, transfer_ref, coupling_ref, send_ref, cluster_ref, coeff_ref, count_ref)


def last_body(recv_ref, spread_ref, base_ref, target_ref, out_ref):
    finish(recv_ref, spread_ref, base_ref, target_ref, out_ref)


def shape(*dims, dtype=BF16):
    return jax.ShapeDtypeStruct(dims, dtype)


def shards(
    density, panels, near_mask, source_basis, leaf_transfer, cluster_coupling,
    out_leaf, out_wide, out_target, coupling, target_basis,
):
    panels_here = LEAVES * LEAF_SIZE
    swap = [(0, 1), (1, 0)]
    code = out_wide[:, 0] * 16 + out_target * 4 + out_leaf
    work = [pltpu.VMEM((LEAVES * RIGHT_SIDES, RANK), BF16), pltpu.SMEM((NZ * NY,), jnp.int32)]
    sends = [shape(NY, CHUNK, 128), shape(NARROW, RIGHT_SIDES, 128)]
    values = shape(RIGHT_SIDES, panels_here)

    def exchange(block, axis):
        return lax.all_to_all(block, axis, 0, 0, tiled=True)

    merge = call(merge_body, "merge", [shape(NZ, LEAVES * ROWS, 128)], [VM])
    nearby = call(
        near_body, "nearby",
        [shape(RIGHT_SIDES, panels_here, dtype=F32), shape(LEAVES * ROWS, 128, dtype=F32)], [VM] * 6,
    )

    other_panels = lax.ppermute(panels, "c", swap)
    other = lax.ppermute(density, "c", swap)
    send, cluster = call(first_body, "first", sends, [VM, SM, VM, VM, VM], work)(
        density, code, source_basis, leaf_transfer, coupling
    )
    arrived = exchange(send, "y")
    group = exchange(cluster, ("x", "c"))
    merged = merge(arrived)[0]
    received = exchange(merged, "z")
    kernel = call(kernel_body, "kernel", [shape(panels_here, 2 * panels_here)], [VM, VM, SM])(
        panels, other_panels, near_mask
    )[0]
    base, spread = nearby(density, other, kernel, group, cluster_coupling, leaf_transfer)
    first_pass, send, cluster = call(
        middle_body, "middle", [values] + sends, [VM, VM, VM, VM, SM, VM, VM, VM], work
    )(received, spread, base, target_basis, code, source_basis, leaf_transfer, coupling)

    arrived = exchange(send, "y")
    group = exchange(cluster, ("x", "c"))
    other = lax.ppermute(first_pass, "c", swap)
    merged = merge(arrived)[0]
    received = exchange(merged, "z")
    base, spread = nearby(first_pass, other, kernel, group, cluster_coupling, leaf_transfer)
    second_pass = call(last_body, "last", [values], [VM] * 4)(received, spread, base, target_basis)[0]
    return (first_pass, second_pass)


def solution(mesh):
    grid = Mesh(np.asarray(mesh.devices).reshape(NZ, NY, NX, NC), ("z", "y", "x", "c"))
    every = ("z", "y", "x", "c")
    cols, rows = P(None, every), P(every)
    in_specs = (cols, cols, rows, cols, rows, rows, rows, rows, rows, rows, cols)
    return jax.shard_map(shards, mesh=grid, in_specs=in_specs, out_specs=(cols, cols), check_vma=False)
```

```python
import math

import jax
import jax.numpy as jnp
import numpy as np
from jax import lax
from jax.experimental import pallas as pl
from jax.experimental.pallas import tpu as pltpu
from jax.sharding import Mesh, PartitionSpec as P

LEAF_SIZE = 128
RANK = 64
RIGHT_SIDES = 32
LEAVES = 4
OUTS = 64
SMOOTHING = 0.0625
NA, NB, NY, NX, NC = 8, 2, 4, 4, 2
PEERS = NB * NY
SLOTS = 2 * NA
ROWS = 16
CHUNK = SLOTS * ROWS + SLOTS
EMPTY = 4
F32, BF16 = jnp.float32, jnp.bfloat16
NT = (((1,), (1,)), ((), ()))


def call(body, name, out_shape, in_spaces, scratch=(), out_spaces=None):
    return pl.pallas_call(
        body,
        out_shape=out_shape,
        in_specs=[pl.BlockSpec(memory_space=space) for space in in_spaces],
        out_specs=[pl.BlockSpec(memory_space=space) for space in out_spaces or [pltpu.VMEM] * len(out_shape)],
        scratch_shapes=list(scratch),
        compiler_params=pltpu.CompilerParams(vmem_limit_bytes=32 * 1024 * 1024),
        name=name,
    )


VM, SM = pltpu.VMEM, pltpu.SMEM


def dot(a, b, dims=None):
    if dims is None:
        return jnp.dot(a, b, preferred_element_type=F32)
    return lax.dot_general(a, b, dims, preferred_element_type=F32)


def pack(block):
    return jnp.concatenate([block[:ROWS], block[ROWS:]], axis=1)


def leaf_cols(leaf):
    return slice(leaf * LEAF_SIZE, (leaf + 1) * LEAF_SIZE)


def leaf_coeffs(value_ref, basis_ref, transfer_ref, swap_ref, coeff_ref):
    cluster = jnp.zeros((RIGHT_SIDES, RANK), F32)
    for leaf in range(LEAVES):
        coeff = dot(value_ref[:, leaf_cols(leaf)], basis_ref[:, leaf_cols(leaf)], NT).astype(BF16)
        coeff_ref[leaf * RIGHT_SIDES : (leaf + 1) * RIGHT_SIDES, :] = coeff
        cluster += dot(coeff, transfer_ref[leaf])
    swap_ref[:, : LEAVES * LEAF_SIZE] = value_ref[...]
    swap_ref[:, LEAVES * LEAF_SIZE :] = jnp.concatenate([cluster, jnp.zeros_like(cluster)], axis=1).astype(BF16)


def product(block, place_ref, coupling_ref, coeff_ref, send_ref):
    place = place_ref[block]
    source = place % 4
    slot = (place // 16) % SLOTS
    peer = place // (16 * SLOTS)
    coeff = coeff_ref[pl.ds(pl.multiple_of(source * RIGHT_SIDES, RIGHT_SIDES), RIGHT_SIDES), :]
    packed = pack(dot(coeff, coupling_ref[block])).astype(BF16)
    send_ref[peer, pl.ds(pl.multiple_of(slot * ROWS, ROWS), ROWS), :] = packed


def clear(send_ref):
    for peer in range(PEERS):
        send_ref[peer, : SLOTS * ROWS, :] = jnp.zeros((SLOTS * ROWS, 128), BF16)


def first_body(
    leaf_ref, wide_ref, target_ref, value_hbm, basis_hbm, transfer_hbm, coupling_hbm,
    send_ref, swap_ref, ids_ref, place_ref,
    value_ref, basis_ref, transfer_ref, coupling_ref, coeff_ref, row_ref, count_ref, sems,
):
    copies = [
        pltpu.make_async_copy(value_hbm, value_ref, sems.at[0]),
        pltpu.make_async_copy(basis_hbm, basis_ref, sems.at[1]),
        pltpu.make_async_copy(transfer_hbm, transfer_ref, sems.at[2]),
    ]
    parts = 4
    each = OUTS // parts
    for part in range(parts):
        span = pl.ds(part * each, each)
        copies.append(pltpu.make_async_copy(coupling_hbm.at[span], coupling_ref.at[span], sems.at[3 + part]))
    for copy in copies:
        copy.start()
    for wide in range(NA * PEERS):
        count_ref[wide] = 0
    row_ref[...] = jnp.full((PEERS * SLOTS, 128), EMPTY, F32)
    clear(send_ref)
    for block in range(OUTS):
        wide = wide_ref[block]
        target = target_ref[block]
        turn = count_ref[wide]
        count_ref[wide] = turn + 1
        spot = (wide % PEERS) * SLOTS + (wide // PEERS) * 2 + turn
        place_ref[block] = spot * 16 + target * 4 + leaf_ref[block]
        row_ref[pl.ds(spot, 1), :] = jnp.full((1, 128), target, jnp.int32).astype(F32)
    for peer in range(PEERS):
        ids = row_ref[peer * SLOTS : (peer + 1) * SLOTS, :].astype(BF16)
        ids_ref[peer] = ids
        send_ref[peer, SLOTS * ROWS :, :] = ids
    for copy in copies[:3]:
        copy.wait()
    leaf_coeffs(value_ref, basis_ref, transfer_ref, swap_ref, coeff_ref)
    for part in range(parts):
        copies[3 + part].wait()
        for block in range(part * each, (part + 1) * each):
            product(block, place_ref, coupling_ref, coeff_ref, send_ref)


def merge_body(recv_ref, out_ref):
    ids = [recv_ref[src, SLOTS * ROWS :, :].astype(F32) for src in range(PEERS)]
    for pair in range(NA):
        total = [jnp.zeros((ROWS, 128), F32) for _ in range(LEAVES)]
        for src in range(PEERS):
            for turn in range(2):
                slot = pair * 2 + turn
                block = recv_ref[src, slot * ROWS : (slot + 1) * ROWS, :].astype(F32)
                row = jnp.broadcast_to(ids[src][slot : slot + 1, :], (ROWS, 128))
                for leaf in range(LEAVES):
                    total[leaf] += jnp.where(row == leaf, block, 0.0)
        for leaf in range(LEAVES):
            out_ref[pair, leaf * ROWS : (leaf + 1) * ROWS, :] = total[leaf].astype(BF16)


def kernel_body(own_ref, other_ref, mask_ref, kernel_ref):
    columns = jnp.transpose(
        jnp.concatenate([own_ref[0:3, :], jnp.zeros((5, LEAVES * LEAF_SIZE), F32)], axis=0)
    )
    for leaf in range(LEAVES):
        place = [columns[leaf_cols(leaf), axis : axis + 1] for axis in range(3)]
        for side, ref in enumerate((own_ref, other_ref)):
            for near in range(max(leaf - 1, 0), min(leaf + 2, LEAVES)):
                source = [ref[row : row + 1, leaf_cols(near)] for row in range(7)]
                offset = [place[axis] - source[axis] for axis in range(3)]
                squared = offset[0] * offset[0] + offset[1] * offset[1] + offset[2] * offset[2] + SMOOTHING
                along = offset[0] * source[3] + offset[1] * source[4] + offset[2] * source[5]
                inverse = lax.rsqrt(squared)
                kernel = (source[6] * (1.0 / (4.0 * math.pi))) * along * (inverse * inverse * inverse)
                keep = mask_ref[leaf, side * LEAVES + near] != 0
                first = side * LEAVES * LEAF_SIZE
                kernel_ref[leaf_cols(leaf), first + near * LEAF_SIZE : first + (near + 1) * LEAF_SIZE] = jnp.where(
                    keep, kernel, 0.0
                ).astype(BF16)


def near_body(value_ref, other_ref, kernel_ref, two_ref, four_ref, eight_ref, rows_ref, transfer_ref, base_ref, spread_ref):
    width = LEAVES * LEAF_SIZE
    for leaf in range(LEAVES):
        low, high = max(leaf - 1, 0) * LEAF_SIZE, min(leaf + 2, LEAVES) * LEAF_SIZE
        near = dot(value_ref[:, low:high], kernel_ref[leaf_cols(leaf), low:high], NT)
        near += dot(other_ref[:, low:high], kernel_ref[leaf_cols(leaf), width + low : width + high], NT)
        base_ref[:, leaf_cols(leaf)] = near + 0.5 * value_ref[:, leaf_cols(leaf)].astype(F32)
    me = lax.axis_index("x") * NC + lax.axis_index("c")
    down = jnp.zeros((RIGHT_SIDES, RANK), F32)
    pairs = [two_ref[...], four_ref[...], eight_ref[:, :128], eight_ref[:, 128:]]
    for step, pair in enumerate(pairs):
        rows = [
            rows_ref[0, pl.ds(pl.multiple_of(jnp.bitwise_xor(me, 2 * step + turn) * RANK, RANK), RANK), :]
            for turn in range(2)
        ]
        down += dot(pair, jnp.concatenate(rows, axis=0))
    high = down.astype(BF16)
    low = (down - high.astype(F32)).astype(BF16)
    for leaf in range(LEAVES):
        spread = dot(high, transfer_ref[leaf], NT) + dot(low, transfer_ref[leaf], NT)
        spread_ref[leaf * ROWS : (leaf + 1) * ROWS, :] = pack(spread)


def finish(recv_ref, spread_ref, base_ref, target_ref, out_ref):
    field = spread_ref[...]
    for src in range(NA):
        field += recv_ref[src].astype(F32)
    field = field.astype(BF16)
    lower = lax.broadcasted_iota(jnp.int32, (ROWS, 128), 1) < RANK
    for leaf in range(LEAVES):
        block = field[leaf * ROWS : (leaf + 1) * ROWS, :].astype(F32)
        tall = jnp.concatenate([jnp.where(lower, block, 0.0), jnp.where(lower, 0.0, block)], axis=0).astype(BF16)
        basis = target_ref[:, leaf_cols(leaf)]
        far = dot(tall, jnp.concatenate([basis, basis], axis=0))
        out_ref[:, leaf_cols(leaf)] = (base_ref[:, leaf_cols(leaf)] + far).astype(BF16)


def middle_body(
    recv_ref, spread_ref, base_ref, target_ref, place_ref, ids_ref, basis_ref, transfer_ref, coupling_ref,
    out_ref, send_ref, swap_ref, coeff_ref,
):
    finish(recv_ref, spread_ref, base_ref, target_ref, out_ref)
    clear(send_ref)
    for peer in range(PEERS):
        send_ref[peer, SLOTS * ROWS :, :] = ids_ref[peer]
    leaf_coeffs(out_ref, basis_ref, transfer_ref, swap_ref, coeff_ref)
    for block in range(OUTS):
        product(block, place_ref, coupling_ref, coeff_ref, send_ref)


def last_body(recv_ref, spread_ref, base_ref, target_ref, out_ref):
    finish(recv_ref, spread_ref, base_ref, target_ref, out_ref)


def shape(*dims, dtype=BF16):
    return jax.ShapeDtypeStruct(dims, dtype)


def shards(
    density, panels, near_mask, source_basis, leaf_transfer, cluster_coupling,
    out_leaf, out_wide, out_target, coupling, target_basis,
):
    panels_here = LEAVES * LEAF_SIZE
    values = shape(RIGHT_SIDES, panels_here)
    sends = [shape(PEERS, CHUNK, 128), shape(RIGHT_SIDES, panels_here + 128)]
    coeff_work = pltpu.VMEM((LEAVES * RIGHT_SIDES, RANK), BF16)

    def swap(block, axis, distance):
        count = lax.axis_size(axis)
        return lax.ppermute(block, axis, [(i, i ^ distance) for i in range(count)])

    first = call(
        first_body, "first", sends + [shape(PEERS, SLOTS, 128), shape(OUTS, dtype=jnp.int32)],
        [SM] * 3 + [pl.ANY] * 4,
        [
            pltpu.VMEM((RIGHT_SIDES, panels_here), BF16),
            pltpu.VMEM((RANK, panels_here), BF16),
            pltpu.VMEM((LEAVES, RANK, RANK), BF16),
            pltpu.VMEM((OUTS, RANK, RANK), BF16),
            coeff_work,
            pltpu.VMEM((PEERS * SLOTS, 128), F32),
            pltpu.SMEM((NA * PEERS,), jnp.int32),
            pltpu.SemaphoreType.DMA((7,)),
        ],
        [VM, VM, VM, SM],
    )
    merge = call(merge_body, "merge", [shape(NA, LEAVES * ROWS, 128)], [VM])
    nearby = call(
        near_body, "nearby",
        [shape(RIGHT_SIDES, panels_here, dtype=F32), shape(LEAVES * ROWS, 128, dtype=F32)], [VM] * 8,
    )

    def couple(send):
        arrived = lax.all_to_all(send, ("b", "y"), 0, 0, tiled=True)
        return lax.all_to_all(merge(arrived)[0], "a", 0, 0, tiled=True)

    def local(value, packet, kernel):
        other = swap(packet, "c", 1)
        two = jnp.concatenate([packet[:, panels_here : panels_here + RANK], other[:, panels_here : panels_here + RANK]], axis=1)
        four = swap(two, "x", 1)
        eight = swap(jnp.concatenate([two, four], axis=1), "x", 2)
        return nearby(value, other, kernel, two, four, eight, cluster_coupling, leaf_transfer)

    send, packet, ids, place = first(
        out_leaf, out_wide.reshape(OUTS), out_target, density, source_basis, leaf_transfer, coupling
    )
    received = couple(send)
    kernel = call(kernel_body, "kernel", [shape(panels_here, 2 * panels_here)], [VM, VM, SM])(
        panels, swap(panels, "c", 1), near_mask
    )[0]
    base, spread = local(density, packet, kernel)
    first_pass, send, packet = call(
        middle_body, "middle", [values] + sends, [VM, VM, VM, VM, SM, VM, VM, VM, VM], [coeff_work]
    )(received, spread, base, target_basis, place, ids, source_basis, leaf_transfer, coupling)

    received = couple(send)
    base, spread = local(first_pass, packet, kernel)
    second_pass = call(last_body, "last", [values], [VM] * 4)(received, spread, base, target_basis)[0]
    return (first_pass, second_pass)


def solution(mesh):
    every = ("a", "b", "y", "x", "c")
    grid = Mesh(np.asarray(mesh.devices).reshape(NA, NB, NY, NX, NC), every)
    cols, rows = P(None, every), P(every)
    in_specs = (cols, cols, rows, cols, rows, rows, rows, rows, rows, rows, cols)
    return jax.shard_map(shards, mesh=grid, in_specs=in_specs, out_specs=(cols, cols), check_vma=False)
```

```python
import math

import jax
import jax.numpy as jnp
import numpy as np
from jax import lax
from jax.experimental import pallas as pl
from jax.experimental.pallas import tpu as pltpu
from jax.sharding import Mesh, PartitionSpec as P

LEAF_SIZE = 128
RANK = 64
RIGHT_SIDES = 32
LEAVES = 4
OUTS = 64
SMOOTHING = 0.0625
NA, NB, NY, NX, NC = 8, 2, 4, 4, 2
PEERS = NB * NY
SLOTS = 2 * NA
ROWS = 16
CHUNK = SLOTS * ROWS + SLOTS
PARTS = 3
EMPTY = 4
F32, BF16 = jnp.float32, jnp.bfloat16
NT = (((1,), (1,)), ((), ()))


def call(body, name, out_shape, in_spaces, scratch=(), out_spaces=None):
    return pl.pallas_call(
        body,
        out_shape=out_shape,
        in_specs=[pl.BlockSpec(memory_space=space) for space in in_spaces],
        out_specs=[pl.BlockSpec(memory_space=space) for space in out_spaces or [pltpu.VMEM] * len(out_shape)],
        scratch_shapes=list(scratch),
        compiler_params=pltpu.CompilerParams(vmem_limit_bytes=32 * 1024 * 1024),
        name=name,
    )


VM, SM = pltpu.VMEM, pltpu.SMEM


def dot(a, b, dims=None):
    if dims is None:
        return jnp.dot(a, b, preferred_element_type=F32)
    return lax.dot_general(a, b, dims, preferred_element_type=F32)


def pack(block):
    return jnp.concatenate([block[:ROWS], block[ROWS:]], axis=1)


def leaf_cols(leaf):
    return slice(leaf * LEAF_SIZE, (leaf + 1) * LEAF_SIZE)


def split_parts(value):
    high = value.astype(BF16)
    rest = value - high.astype(F32)
    middle = rest.astype(BF16)
    return high, middle, (rest - middle.astype(F32)).astype(BF16)


def leaf_coeffs(value_ref, basis_ref, transfer_ref, swap_ref, coeff_ref):
    cluster = jnp.zeros((RIGHT_SIDES, RANK), F32)
    for leaf in range(LEAVES):
        coeff = dot(value_ref[:, leaf_cols(leaf)], basis_ref[:, leaf_cols(leaf)], NT).astype(BF16)
        coeff_ref[leaf * RIGHT_SIDES : (leaf + 1) * RIGHT_SIDES, :] = coeff
        cluster += dot(coeff, transfer_ref[leaf])
    swap_ref[:RIGHT_SIDES, : LEAVES * LEAF_SIZE] = value_ref[...]
    swap_ref[:RIGHT_SIDES, LEAVES * LEAF_SIZE :] = jnp.concatenate([cluster, jnp.zeros_like(cluster)], axis=1).astype(BF16)


def product(block, place_ref, coupling_ref, coeff_ref, send_ref):
    place = place_ref[block]
    source = place % 4
    slot = (place // 16) % SLOTS
    peer = place // (16 * SLOTS)
    coeff = coeff_ref[pl.ds(pl.multiple_of(source * RIGHT_SIDES, RIGHT_SIDES), RIGHT_SIDES), :]
    packed = pack(dot(coeff, coupling_ref[block])).astype(BF16)
    send_ref[peer, pl.ds(pl.multiple_of(slot * ROWS, ROWS), ROWS), :] = packed


def clear(send_ref):
    for peer in range(PEERS):
        send_ref[peer, : SLOTS * ROWS, :] = jnp.zeros((SLOTS * ROWS, 128), BF16)


def first_body(
    leaf_ref, wide_ref, target_ref, panel_hbm, value_hbm, basis_hbm, transfer_hbm, coupling_hbm,
    send_ref, swap_ref, ids_ref, place_ref,
    panel_ref, value_ref, basis_ref, transfer_ref, coupling_ref, coeff_ref, row_ref, count_ref, sems,
):
    copies = [
        pltpu.make_async_copy(value_hbm, value_ref, sems.at[0]),
        pltpu.make_async_copy(basis_hbm, basis_ref, sems.at[1]),
        pltpu.make_async_copy(transfer_hbm, transfer_ref, sems.at[2]),
        pltpu.make_async_copy(panel_hbm, panel_ref, sems.at[3]),
    ]
    parts = 4
    each = OUTS // parts
    for part in range(parts):
        span = pl.ds(part * each, each)
        copies.append(pltpu.make_async_copy(coupling_hbm.at[span], coupling_ref.at[span], sems.at[4 + part]))
    for copy in copies:
        copy.start()
    for wide in range(NA * PEERS):
        count_ref[wide] = 0
    row_ref[...] = jnp.full((PEERS * SLOTS, 128), EMPTY, F32)
    clear(send_ref)
    for block in range(OUTS):
        wide = wide_ref[block]
        target = target_ref[block]
        turn = count_ref[wide]
        count_ref[wide] = turn + 1
        spot = (wide % PEERS) * SLOTS + (wide // PEERS) * 2 + turn
        place_ref[block] = spot * 16 + target * 4 + leaf_ref[block]
        row_ref[pl.ds(spot, 1), :] = jnp.full((1, 128), target, jnp.int32).astype(F32)
    for peer in range(PEERS):
        ids = row_ref[peer * SLOTS : (peer + 1) * SLOTS, :].astype(BF16)
        ids_ref[peer] = ids
        send_ref[peer, SLOTS * ROWS :, :] = ids
    for copy in copies[:4]:
        copy.wait()
    leaf_coeffs(value_ref, basis_ref, transfer_ref, swap_ref, coeff_ref)
    swap_ref[RIGHT_SIDES:, :] = jnp.zeros((PARTS * ROWS, LEAVES * LEAF_SIZE + 128), BF16)
    panel = jnp.concatenate([panel_ref[...], jnp.zeros((ROWS - 7, LEAVES * LEAF_SIZE), F32)], axis=0)
    for part, rows in enumerate(split_parts(panel)):
        start = RIGHT_SIDES + part * ROWS
        swap_ref[start : start + ROWS, : LEAVES * LEAF_SIZE] = rows
    for part in range(parts):
        copies[4 + part].wait()
        for block in range(part * each, (part + 1) * each):
            product(block, place_ref, coupling_ref, coeff_ref, send_ref)


def merge_body(recv_ref, out_ref):
    ids = [recv_ref[src, SLOTS * ROWS :, :].astype(F32) for src in range(PEERS)]
    for pair in range(NA):
        total = [jnp.zeros((ROWS, 128), F32) for _ in range(LEAVES)]
        for src in range(PEERS):
            for turn in range(2):
                slot = pair * 2 + turn
                block = recv_ref[src, slot * ROWS : (slot + 1) * ROWS, :].astype(F32)
                row = jnp.broadcast_to(ids[src][slot : slot + 1, :], (ROWS, 128))
                for leaf in range(LEAVES):
                    total[leaf] += jnp.where(row == leaf, block, 0.0)
        for leaf in range(LEAVES):
            out_ref[pair, leaf * ROWS : (leaf + 1) * ROWS, :] = total[leaf].astype(BF16)


def kernel_body(own_ref, packet_ref, mask_ref, kernel_ref, other_ref):
    width = LEAVES * LEAF_SIZE
    start = RIGHT_SIDES
    high, middle, low = [
        packet_ref[start + part * ROWS : start + (part + 1) * ROWS, :width].astype(F32) for part in range(PARTS)
    ]
    other_ref[...] = (high + (middle + low))[:8]
    columns = jnp.transpose(
        jnp.concatenate([own_ref[0:3, :], jnp.zeros((5, LEAVES * LEAF_SIZE), F32)], axis=0)
    )
    for leaf in range(LEAVES):
        place = [columns[leaf_cols(leaf), axis : axis + 1] for axis in range(3)]
        for side, ref in enumerate((own_ref, other_ref)):
            for near in range(max(leaf - 1, 0), min(leaf + 2, LEAVES)):
                source = [ref[row : row + 1, leaf_cols(near)] for row in range(7)]
                offset = [place[axis] - source[axis] for axis in range(3)]
                squared = offset[0] * offset[0] + offset[1] * offset[1] + offset[2] * offset[2] + SMOOTHING
                along = offset[0] * source[3] + offset[1] * source[4] + offset[2] * source[5]
                inverse = lax.rsqrt(squared)
                kernel = (source[6] * (1.0 / (4.0 * math.pi))) * along * (inverse * inverse * inverse)
                keep = mask_ref[leaf, side * LEAVES + near] != 0
                first = side * LEAVES * LEAF_SIZE
                kernel_ref[leaf_cols(leaf), first + near * LEAF_SIZE : first + (near + 1) * LEAF_SIZE] = jnp.where(
                    keep, kernel, 0.0
                ).astype(BF16)


def near_body(value_ref, other_ref, kernel_ref, two_ref, four_ref, eight_ref, rows_ref, transfer_ref, base_ref, spread_ref):
    width = LEAVES * LEAF_SIZE
    for leaf in range(LEAVES):
        low, high = max(leaf - 1, 0) * LEAF_SIZE, min(leaf + 2, LEAVES) * LEAF_SIZE
        near = dot(value_ref[:, low:high], kernel_ref[leaf_cols(leaf), low:high], NT)
        near += dot(other_ref[:RIGHT_SIDES, low:high], kernel_ref[leaf_cols(leaf), width + low : width + high], NT)
        base_ref[:, leaf_cols(leaf)] = near + 0.5 * value_ref[:, leaf_cols(leaf)].astype(F32)
    me = lax.axis_index("x") * NC + lax.axis_index("c")
    down = jnp.zeros((RIGHT_SIDES, RANK), F32)
    pairs = [two_ref[...], four_ref[...], eight_ref[:, :128], eight_ref[:, 128:]]
    for step, pair in enumerate(pairs):
        rows = [
            rows_ref[0, pl.ds(pl.multiple_of(jnp.bitwise_xor(me, 2 * step + turn) * RANK, RANK), RANK), :]
            for turn in range(2)
        ]
        down += dot(pair, jnp.concatenate(rows, axis=0))
    high = down.astype(BF16)
    low = (down - high.astype(F32)).astype(BF16)
    for leaf in range(LEAVES):
        spread = dot(high, transfer_ref[leaf], NT) + dot(low, transfer_ref[leaf], NT)
        spread_ref[leaf * ROWS : (leaf + 1) * ROWS, :] = pack(spread)


def finish(recv_ref, spread_ref, base_ref, target_ref, out_ref):
    field = spread_ref[...]
    for src in range(NA):
        field += recv_ref[src].astype(F32)
    field = field.astype(BF16)
    lower = lax.broadcasted_iota(jnp.int32, (ROWS, 128), 1) < RANK
    for leaf in range(LEAVES):
        block = field[leaf * ROWS : (leaf + 1) * ROWS, :].astype(F32)
        tall = jnp.concatenate([jnp.where(lower, block, 0.0), jnp.where(lower, 0.0, block)], axis=0).astype(BF16)
        basis = target_ref[:, leaf_cols(leaf)]
        far = dot(tall, jnp.concatenate([basis, basis], axis=0))
        out_ref[:, leaf_cols(leaf)] = (base_ref[:, leaf_cols(leaf)] + far).astype(BF16)


def middle_body(
    recv_ref, spread_ref, base_ref, target_ref, place_ref, ids_ref, basis_ref, transfer_ref, coupling_ref,
    out_ref, send_ref, swap_ref, coeff_ref,
):
    finish(recv_ref, spread_ref, base_ref, target_ref, out_ref)
    clear(send_ref)
    for peer in range(PEERS):
        send_ref[peer, SLOTS * ROWS :, :] = ids_ref[peer]
    leaf_coeffs(out_ref, basis_ref, transfer_ref, swap_ref, coeff_ref)
    for block in range(OUTS):
        product(block, place_ref, coupling_ref, coeff_ref, send_ref)


def last_body(recv_ref, spread_ref, base_ref, target_ref, out_ref):
    finish(recv_ref, spread_ref, base_ref, target_ref, out_ref)


def shape(*dims, dtype=BF16):
    return jax.ShapeDtypeStruct(dims, dtype)


def shards(
    density, panels, near_mask, source_basis, leaf_transfer, cluster_coupling,
    out_leaf, out_wide, out_target, coupling, target_basis,
):
    panels_here = LEAVES * LEAF_SIZE
    values = shape(RIGHT_SIDES, panels_here)
    packet_width = panels_here + 128
    send_shape = shape(PEERS, CHUNK, 128)
    coeff_work = pltpu.VMEM((LEAVES * RIGHT_SIDES, RANK), BF16)

    def swap(block, axis, distance):
        count = lax.axis_size(axis)
        return lax.ppermute(block, axis, [(i, i ^ distance) for i in range(count)])

    first = call(
        first_body, "first",
        [
            send_shape, shape(RIGHT_SIDES + PARTS * ROWS, packet_width),
            shape(PEERS, SLOTS, 128), shape(OUTS, dtype=jnp.int32),
        ],
        [SM] * 3 + [pltpu.HBM] * 5,
        [
            pltpu.VMEM((7, panels_here), F32),
            pltpu.VMEM((RIGHT_SIDES, panels_here), BF16),
            pltpu.VMEM((RANK, panels_here), BF16),
            pltpu.VMEM((LEAVES, RANK, RANK), BF16),
            pltpu.VMEM((OUTS, RANK, RANK), BF16),
            coeff_work,
            pltpu.VMEM((PEERS * SLOTS, 128), F32),
            pltpu.SMEM((NA * PEERS,), jnp.int32),
            pltpu.SemaphoreType.DMA((8,)),
        ],
        [VM, VM, VM, SM],
    )
    merge = call(merge_body, "merge", [shape(NA, LEAVES * ROWS, 128)], [VM])
    nearby = call(
        near_body, "nearby",
        [shape(RIGHT_SIDES, panels_here, dtype=F32), shape(LEAVES * ROWS, 128, dtype=F32)], [VM] * 8,
    )

    def together(*arrays):
        return lax.optimization_barrier(arrays)

    def couple(value, send, packet, kernel):
        columns = slice(panels_here, panels_here + RANK)
        arrived = lax.all_to_all(send, ("b", "y"), 0, 0, tiled=True)
        other = swap(packet, "c", 1)
        two = jnp.concatenate([packet[:RIGHT_SIDES, columns], other[:RIGHT_SIDES, columns]], axis=1)
        four = swap(two, "x", 1)
        arrived, four = together(arrived, four)
        merged, four = together(merge(arrived)[0], four)
        received = lax.all_to_all(merged, "a", 0, 0, tiled=True)
        eight = swap(jnp.concatenate([two, four], axis=1), "x", 2)
        if kernel is None:
            kernel = call(
                kernel_body, "kernel", [shape(panels_here, 2 * panels_here)], [VM, VM, SM],
                [pltpu.VMEM((8, panels_here), F32)],
            )(panels, other, near_mask)[0]
        base, spread = nearby(value, other, kernel, two, four, eight, cluster_coupling, leaf_transfer)
        return received, base, spread, kernel

    send, packet, ids, place = first(
        out_leaf, out_wide.reshape(OUTS), out_target, panels, density, source_basis, leaf_transfer, coupling
    )
    received, base, spread, kernel = couple(density, send, packet, None)
    first_pass, send, packet = call(
        middle_body, "middle", [values, send_shape, shape(RIGHT_SIDES, packet_width)],
        [VM, VM, VM, VM, SM, VM, VM, VM, VM], [coeff_work],
    )(received, spread, base, target_basis, place, ids, source_basis, leaf_transfer, coupling)

    received, base, spread, kernel = couple(first_pass, send, packet, kernel)
    second_pass = call(last_body, "last", [values], [VM] * 4)(received, spread, base, target_basis)[0]
    return (first_pass, second_pass)


def solution(mesh):
    every = ("a", "b", "y", "x", "c")
    grid = Mesh(np.asarray(mesh.devices).reshape(NA, NB, NY, NX, NC), every)
    cols, rows = P(None, every), P(every)
    in_specs = (cols, cols, rows, cols, rows, rows, rows, rows, rows, rows, cols)
    return jax.shard_map(shards, mesh=grid, in_specs=in_specs, out_specs=(cols, cols), check_vma=False)
```

```python
import math

import jax
import jax.numpy as jnp
import numpy as np
from jax import lax
from jax.experimental import pallas as pl
from jax.experimental.pallas import tpu as pltpu
from jax.sharding import Mesh, PartitionSpec as P

LEAF_SIZE = 128
RANK = 64
RIGHT_SIDES = 32
LEAVES = 4
OUTS = 64
SMOOTHING = 0.0625
NA, NB, NY, NX, NC = 8, 2, 4, 4, 2
PEERS = NB * NY
SLOTS = 2 * NA
ROWS = 16
CHUNK = SLOTS * ROWS
IDS = 16
PARTS = 3
F32, BF16 = jnp.float32, jnp.bfloat16
NT = (((1,), (1,)), ((), ()))


def call(body, name, out_shape, in_spaces, scratch=(), out_spaces=None):
    return pl.pallas_call(
        body,
        out_shape=out_shape,
        in_specs=[pl.BlockSpec(memory_space=space) for space in in_spaces],
        out_specs=[pl.BlockSpec(memory_space=space) for space in out_spaces or [pltpu.VMEM] * len(out_shape)],
        scratch_shapes=list(scratch),
        compiler_params=pltpu.CompilerParams(vmem_limit_bytes=32 * 1024 * 1024),
        name=name,
    )


VM, SM = pltpu.VMEM, pltpu.SMEM


def dot(a, b, dims=None):
    if dims is None:
        return jnp.dot(a, b, preferred_element_type=F32)
    return lax.dot_general(a, b, dims, preferred_element_type=F32)


def pack(block):
    return jnp.concatenate([block[:ROWS], block[ROWS:]], axis=1)


def leaf_cols(leaf):
    return slice(leaf * LEAF_SIZE, (leaf + 1) * LEAF_SIZE)


def split_parts(value):
    high = value.astype(BF16)
    rest = value - high.astype(F32)
    middle = rest.astype(BF16)
    return high, middle, (rest - middle.astype(F32)).astype(BF16)


def leaf_coeffs(value_ref, basis_ref, transfer_ref, swap_ref, coeff_ref):
    cluster = jnp.zeros((RIGHT_SIDES, RANK), F32)
    for leaf in range(LEAVES):
        coeff = dot(value_ref[:, leaf_cols(leaf)], basis_ref[:, leaf_cols(leaf)], NT).astype(BF16)
        coeff_ref[leaf * RIGHT_SIDES : (leaf + 1) * RIGHT_SIDES, :] = coeff
        cluster += dot(coeff, transfer_ref[leaf])
    swap_ref[:RIGHT_SIDES, : LEAVES * LEAF_SIZE] = value_ref[...]
    swap_ref[:RIGHT_SIDES, LEAVES * LEAF_SIZE :] = jnp.concatenate([cluster, jnp.zeros_like(cluster)], axis=1).astype(BF16)


def product(block, place_ref, coupling_ref, coeff_ref, send_ref):
    place = place_ref[block]
    peer = lax.shift_right_logical(place, 8)
    row = pl.multiple_of(jnp.bitwise_and(place, CHUNK - 1), ROWS)
    source = pl.multiple_of(place_ref[OUTS + block], RIGHT_SIDES)
    packed = pack(dot(coeff_ref[pl.ds(source, RIGHT_SIDES), :], coupling_ref[block])).astype(BF16)
    send_ref[peer, pl.ds(row, ROWS), :] = packed


def clear(send_ref):
    for peer in range(PEERS):
        send_ref[peer, :CHUNK, :] = jnp.zeros((CHUNK, 128), BF16)


def first_body(
    leaf_hbm, wide_hbm, target_hbm, panel_hbm, value_hbm, basis_hbm, transfer_hbm, coupling_hbm,
    send_ref, swap_ref, place_ref,
    leaf_ref, wide_ref, target_ref, panel_ref, value_ref, basis_ref, transfer_ref, coupling_ref,
    coeff_ref, row_ref, count_ref, sems,
):
    pairs = [
        (wide_hbm, wide_ref), (target_hbm, target_ref), (leaf_hbm, leaf_ref),
        (value_hbm, value_ref), (basis_hbm, basis_ref), (transfer_hbm, transfer_ref), (panel_hbm, panel_ref),
    ]
    parts = 4
    each = OUTS // parts
    for part in range(parts):
        span = pl.ds(part * each, each)
        pairs.append((coupling_hbm.at[span], coupling_ref.at[span]))
    copies = [pltpu.make_async_copy(source, place, sems.at[i]) for i, (source, place) in enumerate(pairs)]
    for copy in copies:
        copy.start()
    for wide in range(NA * PEERS):
        count_ref[wide] = 0
    clear(send_ref)
    for copy in copies[:3]:
        copy.wait()
    row_ref[...] = jnp.zeros((2 * PEERS * NA, 128), F32)
    for block in range(OUTS):
        wide = wide_ref[block]
        turn = count_ref[wide]
        count_ref[wide] = turn + 1
        peer = jnp.bitwise_and(wide, PEERS - 1)
        pair = lax.shift_right_logical(wide, 3)
        place_ref[block] = peer * CHUNK + (pair * 2 + turn) * ROWS
        place_ref[OUTS + block] = leaf_ref[block] * RIGHT_SIDES
        spot = turn * (PEERS * NA) + peer * NA + pair
        row_ref[pl.ds(spot, 1), :] = jnp.full((1, 128), target_ref[block] + 1, jnp.int32).astype(F32)
    early = jnp.bitwise_and(lax.broadcasted_iota(jnp.int32, (NA, 128), 1), 2 * ROWS - 1) < ROWS
    for peer in range(PEERS):
        turns = [row_ref[(turn * PEERS + peer) * NA : (turn * PEERS + peer + 1) * NA, :] for turn in range(2)]
        ids = jnp.where(early, turns[0], turns[1])
        send_ref[peer, CHUNK:, :] = jnp.concatenate([ids, ids], axis=0).astype(BF16)
    for copy in copies[3:7]:
        copy.wait()
    leaf_coeffs(value_ref, basis_ref, transfer_ref, swap_ref, coeff_ref)
    swap_ref[RIGHT_SIDES:, :] = jnp.zeros((PARTS * ROWS, LEAVES * LEAF_SIZE + 128), BF16)
    panel = jnp.concatenate([panel_ref[...], jnp.zeros((ROWS - 7, LEAVES * LEAF_SIZE), F32)], axis=0)
    for part, rows in enumerate(split_parts(panel)):
        start = RIGHT_SIDES + part * ROWS
        swap_ref[start : start + ROWS, : LEAVES * LEAF_SIZE] = rows
    for part in range(parts):
        copies[7 + part].wait()
        for block in range(part * each, (part + 1) * each):
            product(block, place_ref, coupling_ref, coeff_ref, send_ref)


def merge(recv_ref, choice_ref, out_ref):
    for pair in range(NA):
        blocks = [recv_ref[src, pair * 2 * ROWS : (pair + 1) * 2 * ROWS, :] for src in range(PEERS)]
        out_ref[pair] = dot(choice_ref[pair], jnp.concatenate(blocks, axis=0)).astype(BF16)


def first_merge_body(recv_ref, out_ref, choice_ref):
    group = lax.shift_right_logical(lax.broadcasted_iota(jnp.int32, (NA, 128), 1), 5)
    halves = []
    for half in range(2):
        ids = jnp.zeros((NA, 128), F32)
        for src in range(4):
            rows = recv_ref[half * 4 + src, CHUNK : CHUNK + IDS, :].astype(F32)[:NA]
            ids += jnp.where(group == src, rows, 0.0)
        halves.append(ids)
    ids = jnp.concatenate(halves, axis=1)
    dims = (LEAVES * ROWS, 2 * 128)
    row, lane = lax.broadcasted_iota(jnp.int32, dims, 0), lax.broadcasted_iota(jnp.int32, dims, 1)
    same = jnp.bitwise_and(row, ROWS - 1) == jnp.bitwise_and(lane, ROWS - 1)
    wanted = jnp.where(same, lax.shift_right_logical(row, 4) + 1, -1).astype(F32)
    for pair in range(NA):
        here = jnp.broadcast_to(ids[pair : pair + 1, :], dims)
        choice_ref[pair] = jnp.where(here == wanted, 1.0, 0.0).astype(BF16)
    merge(recv_ref, choice_ref, out_ref)


def merge_body(recv_ref, choice_ref, out_ref):
    merge(recv_ref, choice_ref, out_ref)


def kernel_body(own_ref, packet_ref, mask_ref, kernel_ref, other_ref):
    width = LEAVES * LEAF_SIZE
    start = RIGHT_SIDES
    high, middle, low = [
        packet_ref[start + part * ROWS : start + (part + 1) * ROWS, :width].astype(F32) for part in range(PARTS)
    ]
    other_ref[...] = (high + (middle + low))[:8]
    columns = jnp.transpose(
        jnp.concatenate([own_ref[0:3, :], jnp.zeros((5, LEAVES * LEAF_SIZE), F32)], axis=0)
    )
    for leaf in range(LEAVES):
        place = [columns[leaf_cols(leaf), axis : axis + 1] for axis in range(3)]
        for side, ref in enumerate((own_ref, other_ref)):
            for near in range(max(leaf - 1, 0), min(leaf + 2, LEAVES)):
                source = [ref[row : row + 1, leaf_cols(near)] for row in range(7)]
                offset = [place[axis] - source[axis] for axis in range(3)]
                squared = offset[0] * offset[0] + offset[1] * offset[1] + offset[2] * offset[2] + SMOOTHING
                along = offset[0] * source[3] + offset[1] * source[4] + offset[2] * source[5]
                inverse = lax.rsqrt(squared)
                kernel = (source[6] * (1.0 / (4.0 * math.pi))) * along * (inverse * inverse * inverse)
                keep = mask_ref[leaf, side * LEAVES + near] != 0
                first = side * LEAVES * LEAF_SIZE
                kernel_ref[leaf_cols(leaf), first + near * LEAF_SIZE : first + (near + 1) * LEAF_SIZE] = jnp.where(
                    keep, kernel, 0.0
                ).astype(BF16)


def near_body(value_ref, other_ref, kernel_ref, two_ref, four_ref, eight_ref, rows_ref, transfer_ref, base_ref, spread_ref):
    width = LEAVES * LEAF_SIZE
    for leaf in range(LEAVES):
        low, high = max(leaf - 1, 0) * LEAF_SIZE, min(leaf + 2, LEAVES) * LEAF_SIZE
        near = dot(value_ref[:, low:high], kernel_ref[leaf_cols(leaf), low:high], NT)
        near += dot(other_ref[:RIGHT_SIDES, low:high], kernel_ref[leaf_cols(leaf), width + low : width + high], NT)
        base_ref[:, leaf_cols(leaf)] = near + 0.5 * value_ref[:, leaf_cols(leaf)].astype(F32)
    me = lax.axis_index("x") * NC + lax.axis_index("c")
    down = jnp.zeros((RIGHT_SIDES, RANK), F32)
    pairs = [two_ref[...], four_ref[...], eight_ref[:, :128], eight_ref[:, 128:]]
    for step, pair in enumerate(pairs):
        rows = [
            rows_ref[0, pl.ds(pl.multiple_of(jnp.bitwise_xor(me, 2 * step + turn) * RANK, RANK), RANK), :]
            for turn in range(2)
        ]
        down += dot(pair, jnp.concatenate(rows, axis=0))
    high = down.astype(BF16)
    low = (down - high.astype(F32)).astype(BF16)
    for leaf in range(LEAVES):
        spread = dot(high, transfer_ref[leaf], NT) + dot(low, transfer_ref[leaf], NT)
        spread_ref[leaf * ROWS : (leaf + 1) * ROWS, :] = pack(spread)


def finish(recv_ref, spread_ref, base_ref, target_ref, out_ref):
    field = spread_ref[...]
    for src in range(NA):
        field += recv_ref[src].astype(F32)
    field = field.astype(BF16)
    lower = lax.broadcasted_iota(jnp.int32, (ROWS, 128), 1) < RANK
    for leaf in range(LEAVES):
        block = field[leaf * ROWS : (leaf + 1) * ROWS, :].astype(F32)
        tall = jnp.concatenate([jnp.where(lower, block, 0.0), jnp.where(lower, 0.0, block)], axis=0).astype(BF16)
        basis = target_ref[:, leaf_cols(leaf)]
        far = dot(tall, jnp.concatenate([basis, basis], axis=0))
        out_ref[:, leaf_cols(leaf)] = (base_ref[:, leaf_cols(leaf)] + far).astype(BF16)


def middle_body(
    recv_ref, spread_ref, base_ref, target_ref, place_ref, basis_ref, transfer_ref, coupling_ref,
    out_ref, send_ref, swap_ref, coeff_ref,
):
    finish(recv_ref, spread_ref, base_ref, target_ref, out_ref)
    clear(send_ref)
    leaf_coeffs(out_ref, basis_ref, transfer_ref, swap_ref, coeff_ref)
    for block in range(OUTS):
        product(block, place_ref, coupling_ref, coeff_ref, send_ref)


def last_body(recv_ref, spread_ref, base_ref, target_ref, out_ref):
    finish(recv_ref, spread_ref, base_ref, target_ref, out_ref)


def shape(*dims, dtype=BF16):
    return jax.ShapeDtypeStruct(dims, dtype)


def shards(
    density, panels, near_mask, source_basis, leaf_transfer, cluster_coupling,
    out_leaf, out_wide, out_target, coupling, target_basis,
):
    panels_here = LEAVES * LEAF_SIZE
    values = shape(RIGHT_SIDES, panels_here)
    packet_width = panels_here + 128
    merged_shape = shape(NA, LEAVES * ROWS, 128)
    coeff_work = pltpu.VMEM((LEAVES * RIGHT_SIDES, RANK), BF16)

    def swap(block, axis, distance):
        count = lax.axis_size(axis)
        return lax.ppermute(block, axis, [(i, i ^ distance) for i in range(count)])

    first = call(
        first_body, "first",
        [
            shape(PEERS, CHUNK + IDS, 128), shape(RIGHT_SIDES + PARTS * ROWS, packet_width),
            shape(2 * OUTS, dtype=jnp.int32),
        ],
        [pltpu.HBM] * 8,
        [
            pltpu.SMEM((OUTS,), jnp.int32),
            pltpu.SMEM((OUTS,), jnp.int32),
            pltpu.SMEM((OUTS,), jnp.int32),
            pltpu.VMEM((7, panels_here), F32),
            pltpu.VMEM((RIGHT_SIDES, panels_here), BF16),
            pltpu.VMEM((RANK, panels_here), BF16),
            pltpu.VMEM((LEAVES, RANK, RANK), BF16),
            pltpu.VMEM((OUTS, RANK, RANK), BF16),
            coeff_work,
            pltpu.VMEM((2 * PEERS * NA, 128), F32),
            pltpu.SMEM((NA * PEERS,), jnp.int32),
            pltpu.SemaphoreType.DMA((11,)),
        ],
        [VM, VM, SM],
    )
    first_merge = call(
        first_merge_body, "first_merge", [merged_shape, shape(NA, LEAVES * ROWS, 2 * 128)], [VM]
    )
    next_merge = call(merge_body, "merge", [merged_shape], [VM] * 2)
    nearby = call(
        near_body, "nearby",
        [shape(RIGHT_SIDES, panels_here, dtype=F32), shape(LEAVES * ROWS, 128, dtype=F32)], [VM] * 8,
    )

    def together(*arrays):
        return lax.optimization_barrier(arrays)

    def couple(value, send, packet, choice, kernel):
        columns = slice(panels_here, panels_here + RANK)
        arrived = lax.all_to_all(send, ("b", "y"), 0, 0, tiled=True)
        other = swap(packet, "c", 1)
        two = jnp.concatenate([packet[:RIGHT_SIDES, columns], other[:RIGHT_SIDES, columns]], axis=1)
        four = swap(two, "x", 1)
        arrived, four = together(arrived, four)
        if choice is None:
            merged, choice = first_merge(arrived)
        else:
            merged = next_merge(arrived, choice)[0]
        merged, four = together(merged, four)
        received = lax.all_to_all(merged, "a", 0, 0, tiled=True)
        eight = swap(jnp.concatenate([two, four], axis=1), "x", 2)
        if kernel is None:
            kernel = call(
                kernel_body, "kernel", [shape(panels_here, 2 * panels_here)], [VM, VM, SM],
                [pltpu.VMEM((8, panels_here), F32)],
            )(panels, other, near_mask)[0]
        base, spread = nearby(value, other, kernel, two, four, eight, cluster_coupling, leaf_transfer)
        return received, base, spread, choice, kernel

    operands = (
        out_leaf, out_wide.reshape(OUTS), out_target, panels, density, source_basis, leaf_transfer, coupling
    )
    send, packet, place = first(*[pltpu.with_memory_space_constraint(array, pltpu.HBM) for array in operands])
    received, base, spread, choice, kernel = couple(density, send, packet, None, None)
    first_pass, send, packet = call(
        middle_body, "middle", [values, shape(PEERS, CHUNK, 128), shape(RIGHT_SIDES, packet_width)],
        [VM, VM, VM, VM, SM, VM, VM, VM], [coeff_work],
    )(received, spread, base, target_basis, place, source_basis, leaf_transfer, coupling)

    received, base, spread, choice, kernel = couple(first_pass, send, packet, choice, kernel)
    second_pass = call(last_body, "last", [values], [VM] * 4)(received, spread, base, target_basis)[0]
    return (first_pass, second_pass)


def solution(mesh):
    every = ("a", "b", "y", "x", "c")
    grid = Mesh(np.asarray(mesh.devices).reshape(NA, NB, NY, NX, NC), every)
    cols, rows = P(None, every), P(every)
    in_specs = (cols, cols, rows, cols, rows, rows, rows, rows, rows, rows, cols)
    return jax.shard_map(shards, mesh=grid, in_specs=in_specs, out_specs=(cols, cols), check_vma=False)
```

```python
import math

import jax
import jax.numpy as jnp
import numpy as np
from jax import lax
from jax.experimental import pallas as pl
from jax.experimental.pallas import tpu as pltpu
from jax.sharding import Mesh, PartitionSpec as P

LEAF_SIZE = 128
RANK = 64
RIGHT_SIDES = 32
LEAVES = 4
OUTS = 64
SMOOTHING = 0.0625
NA, NB, NY, NX, NC = 8, 2, 4, 4, 2
PEERS = NB * NY
SLOTS = 2 * NA
ROWS = 16
CHUNK = SLOTS * ROWS
IDS = 16
FIRST_PAIR = 5
ORDER = [(FIRST_PAIR + i) % NA for i in range(NA)]
PARTS = 3
F32, BF16 = jnp.float32, jnp.bfloat16
NT = (((1,), (1,)), ((), ()))


def call(body, name, out_shape, in_spaces, scratch=(), out_spaces=None):
    return pl.pallas_call(
        body,
        out_shape=out_shape,
        in_specs=[pl.BlockSpec(memory_space=space) for space in in_spaces],
        out_specs=[pl.BlockSpec(memory_space=space) for space in out_spaces or [pltpu.VMEM] * len(out_shape)],
        scratch_shapes=list(scratch),
        compiler_params=pltpu.CompilerParams(vmem_limit_bytes=32 * 1024 * 1024),
        name=name,
    )


VM, SM = pltpu.VMEM, pltpu.SMEM


def dot(a, b, dims=None):
    if dims is None:
        return jnp.dot(a, b, preferred_element_type=F32)
    return lax.dot_general(a, b, dims, preferred_element_type=F32)


def pack(block):
    return jnp.concatenate([block[:ROWS], block[ROWS:]], axis=1)


def leaf_cols(leaf):
    return slice(leaf * LEAF_SIZE, (leaf + 1) * LEAF_SIZE)


def split_parts(value):
    high = value.astype(BF16)
    rest = value - high.astype(F32)
    middle = rest.astype(BF16)
    return high, middle, (rest - middle.astype(F32)).astype(BF16)


def leaf_coeffs(value_ref, basis_ref, transfer_ref, swap_ref, coeff_ref):
    cluster = jnp.zeros((RIGHT_SIDES, RANK), F32)
    for leaf in range(LEAVES):
        coeff = dot(value_ref[:, leaf_cols(leaf)], basis_ref[:, leaf_cols(leaf)], NT).astype(BF16)
        coeff_ref[leaf * RIGHT_SIDES : (leaf + 1) * RIGHT_SIDES, :] = coeff
        cluster += dot(coeff, transfer_ref[leaf])
    swap_ref[:RIGHT_SIDES, : LEAVES * LEAF_SIZE] = value_ref[...]
    swap_ref[:RIGHT_SIDES, LEAVES * LEAF_SIZE :] = jnp.concatenate([cluster, jnp.zeros_like(cluster)], axis=1).astype(BF16)


def product(block, place_ref, coupling_ref, coeff_ref, send_ref):
    place = place_ref[block]
    peer = lax.shift_right_logical(place, 8)
    row = pl.multiple_of(jnp.bitwise_and(place, CHUNK - 1), ROWS)
    source = pl.multiple_of(place_ref[OUTS + block], RIGHT_SIDES)
    packed = pack(dot(coeff_ref[pl.ds(source, RIGHT_SIDES), :], coupling_ref[block])).astype(BF16)
    send_ref[peer, pl.ds(row, ROWS), :] = packed


def clear(send_ref):
    for peer in range(PEERS):
        send_ref[peer, :CHUNK, :] = jnp.zeros((CHUNK, 128), BF16)


def first_body(
    leaf_hbm, wide_hbm, target_hbm, panel_hbm, value_hbm, basis_hbm, transfer_hbm, coupling_hbm,
    send_ref, swap_ref, place_ref,
    leaf_ref, wide_ref, target_ref, panel_ref, value_ref, basis_ref, transfer_ref, coupling_ref,
    coeff_ref, row_ref, count_ref, sems,
):
    pairs = [
        (wide_hbm, wide_ref), (target_hbm, target_ref), (leaf_hbm, leaf_ref),
        (value_hbm, value_ref), (basis_hbm, basis_ref), (transfer_hbm, transfer_ref), (panel_hbm, panel_ref),
    ]
    parts = 4
    each = OUTS // parts
    for part in range(parts):
        span = pl.ds(part * each, each)
        pairs.append((coupling_hbm.at[span], coupling_ref.at[span]))
    copies = [pltpu.make_async_copy(source, place, sems.at[i]) for i, (source, place) in enumerate(pairs)]
    for copy in copies:
        copy.start()
    for wide in range(NA * PEERS):
        count_ref[wide] = 0
    clear(send_ref)
    for copy in copies[:3]:
        copy.wait()
    row_ref[...] = jnp.zeros((2 * PEERS * NA, 128), F32)
    for block in range(OUTS):
        wide = wide_ref[block]
        turn = count_ref[wide]
        count_ref[wide] = turn + 1
        peer = jnp.bitwise_and(wide, PEERS - 1)
        pair = lax.shift_right_logical(wide, 3)
        place_ref[block] = peer * CHUNK + (pair * 2 + turn) * ROWS
        place_ref[OUTS + block] = leaf_ref[block] * RIGHT_SIDES
        spot = turn * (PEERS * NA) + peer * NA + pair
        row_ref[pl.ds(spot, 1), :] = jnp.full((1, 128), target_ref[block] + 1, jnp.int32).astype(F32)
    early = jnp.bitwise_and(lax.broadcasted_iota(jnp.int32, (NA, 128), 1), 2 * ROWS - 1) < ROWS
    for peer in range(PEERS):
        turns = [row_ref[(turn * PEERS + peer) * NA : (turn * PEERS + peer + 1) * NA, :] for turn in range(2)]
        ids = jnp.where(early, turns[0], turns[1])
        send_ref[peer, CHUNK:, :] = jnp.concatenate([ids, ids], axis=0).astype(BF16)
    for copy in copies[3:7]:
        copy.wait()
    leaf_coeffs(value_ref, basis_ref, transfer_ref, swap_ref, coeff_ref)
    swap_ref[RIGHT_SIDES:, :] = jnp.zeros((PARTS * ROWS, LEAVES * LEAF_SIZE + 128), BF16)
    panel = jnp.concatenate([panel_ref[...], jnp.zeros((ROWS - 7, LEAVES * LEAF_SIZE), F32)], axis=0)
    for part, rows in enumerate(split_parts(panel)):
        start = RIGHT_SIDES + part * ROWS
        swap_ref[start : start + ROWS, : LEAVES * LEAF_SIZE] = rows
    for part in range(parts):
        copies[7 + part].wait()
        for block in range(part * each, (part + 1) * each):
            product(block, place_ref, coupling_ref, coeff_ref, send_ref)


def merge(recv_ref, choice_ref, out_ref):
    for place, pair in enumerate(ORDER):
        blocks = [recv_ref[src, pair * 2 * ROWS : (pair + 1) * 2 * ROWS, :] for src in range(PEERS)]
        out_ref[place] = dot(choice_ref[pair], jnp.concatenate(blocks, axis=0)).astype(BF16)


def first_merge_body(recv_ref, out_ref, choice_ref):
    group = lax.shift_right_logical(lax.broadcasted_iota(jnp.int32, (NA, 128), 1), 5)
    halves = []
    for half in range(2):
        ids = jnp.zeros((NA, 128), F32)
        for src in range(4):
            rows = recv_ref[half * 4 + src, CHUNK : CHUNK + IDS, :].astype(F32)[:NA]
            ids += jnp.where(group == src, rows, 0.0)
        halves.append(ids)
    ids = jnp.concatenate(halves, axis=1)
    dims = (LEAVES * ROWS, 2 * 128)
    row, lane = lax.broadcasted_iota(jnp.int32, dims, 0), lax.broadcasted_iota(jnp.int32, dims, 1)
    same = jnp.bitwise_and(row, ROWS - 1) == jnp.bitwise_and(lane, ROWS - 1)
    wanted = jnp.where(same, lax.shift_right_logical(row, 4) + 1, -1).astype(F32)
    for pair in range(NA):
        here = jnp.broadcast_to(ids[pair : pair + 1, :], dims)
        choice_ref[pair] = jnp.where(here == wanted, 1.0, 0.0).astype(BF16)
    merge(recv_ref, choice_ref, out_ref)


def merge_body(recv_ref, choice_ref, out_ref):
    merge(recv_ref, choice_ref, out_ref)


def kernel_body(own_ref, packet_ref, mask_ref, kernel_ref, other_ref):
    width = LEAVES * LEAF_SIZE
    start = RIGHT_SIDES
    high, middle, low = [
        packet_ref[start + part * ROWS : start + (part + 1) * ROWS, :width].astype(F32) for part in range(PARTS)
    ]
    other_ref[...] = (high + (middle + low))[:8]
    columns = jnp.transpose(
        jnp.concatenate([own_ref[0:3, :], jnp.zeros((5, LEAVES * LEAF_SIZE), F32)], axis=0)
    )
    for leaf in range(LEAVES):
        place = [columns[leaf_cols(leaf), axis : axis + 1] for axis in range(3)]
        for side, ref in enumerate((own_ref, other_ref)):
            for near in range(max(leaf - 1, 0), min(leaf + 2, LEAVES)):
                source = [ref[row : row + 1, leaf_cols(near)] for row in range(7)]
                offset = [place[axis] - source[axis] for axis in range(3)]
                squared = offset[0] * offset[0] + offset[1] * offset[1] + offset[2] * offset[2] + SMOOTHING
                along = offset[0] * source[3] + offset[1] * source[4] + offset[2] * source[5]
                inverse = lax.rsqrt(squared)
                kernel = (source[6] * (1.0 / (4.0 * math.pi))) * along * (inverse * inverse * inverse)
                keep = mask_ref[leaf, side * LEAVES + near] != 0
                first = side * LEAVES * LEAF_SIZE
                kernel_ref[leaf_cols(leaf), first + near * LEAF_SIZE : first + (near + 1) * LEAF_SIZE] = jnp.where(
                    keep, kernel, 0.0
                ).astype(BF16)


def near_body(value_ref, other_ref, kernel_ref, two_ref, four_ref, eight_ref, rows_ref, transfer_ref, base_ref, spread_ref):
    width = LEAVES * LEAF_SIZE
    for leaf in range(LEAVES):
        low, high = max(leaf - 1, 0) * LEAF_SIZE, min(leaf + 2, LEAVES) * LEAF_SIZE
        near = dot(value_ref[:, low:high], kernel_ref[leaf_cols(leaf), low:high], NT)
        near += dot(other_ref[:RIGHT_SIDES, low:high], kernel_ref[leaf_cols(leaf), width + low : width + high], NT)
        base_ref[:, leaf_cols(leaf)] = near + 0.5 * value_ref[:, leaf_cols(leaf)].astype(F32)
    me = lax.axis_index("x") * NC + lax.axis_index("c")
    down = jnp.zeros((RIGHT_SIDES, RANK), F32)
    pairs = [two_ref[...], four_ref[...], eight_ref[:, :128], eight_ref[:, 128:]]
    for step, pair in enumerate(pairs):
        rows = [
            rows_ref[0, pl.ds(pl.multiple_of(jnp.bitwise_xor(me, 2 * step + turn) * RANK, RANK), RANK), :]
            for turn in range(2)
        ]
        down += dot(pair, jnp.concatenate(rows, axis=0))
    high = down.astype(BF16)
    low = (down - high.astype(F32)).astype(BF16)
    for leaf in range(LEAVES):
        spread = dot(high, transfer_ref[leaf], NT) + dot(low, transfer_ref[leaf], NT)
        spread_ref[leaf * ROWS : (leaf + 1) * ROWS, :] = pack(spread)


def finish(recv_ref, spread_ref, base_ref, target_ref, out_ref):
    field = spread_ref[...]
    for src in range(NA):
        field += recv_ref[src].astype(F32)
    field = field.astype(BF16)
    lower = lax.broadcasted_iota(jnp.int32, (ROWS, 128), 1) < RANK
    for leaf in range(LEAVES):
        block = field[leaf * ROWS : (leaf + 1) * ROWS, :].astype(F32)
        tall = jnp.concatenate([jnp.where(lower, block, 0.0), jnp.where(lower, 0.0, block)], axis=0).astype(BF16)
        basis = target_ref[:, leaf_cols(leaf)]
        far = dot(tall, jnp.concatenate([basis, basis], axis=0))
        out_ref[:, leaf_cols(leaf)] = (base_ref[:, leaf_cols(leaf)] + far).astype(BF16)


def middle_body(
    recv_ref, spread_ref, base_ref, target_ref, place_ref, basis_ref, transfer_ref, coupling_ref,
    out_ref, send_ref, swap_ref, coeff_ref,
):
    finish(recv_ref, spread_ref, base_ref, target_ref, out_ref)
    clear(send_ref)
    leaf_coeffs(out_ref, basis_ref, transfer_ref, swap_ref, coeff_ref)
    for block in range(OUTS):
        product(block, place_ref, coupling_ref, coeff_ref, send_ref)


def last_body(recv_ref, spread_ref, base_ref, target_ref, out_ref):
    finish(recv_ref, spread_ref, base_ref, target_ref, out_ref)


def shape(*dims, dtype=BF16):
    return jax.ShapeDtypeStruct(dims, dtype)


def shards(
    density, panels, near_mask, source_basis, leaf_transfer, cluster_coupling,
    out_leaf, out_wide, out_target, coupling, target_basis,
):
    panels_here = LEAVES * LEAF_SIZE
    values = shape(RIGHT_SIDES, panels_here)
    packet_width = panels_here + 128
    merged_shape = shape(NA, LEAVES * ROWS, 128)
    coeff_work = pltpu.VMEM((LEAVES * RIGHT_SIDES, RANK), BF16)

    def swap(block, axis, distance):
        count = lax.axis_size(axis)
        return lax.ppermute(block, axis, [(i, i ^ distance) for i in range(count)])

    first = call(
        first_body, "first",
        [
            shape(PEERS, CHUNK + IDS, 128), shape(RIGHT_SIDES + PARTS * ROWS, packet_width),
            shape(2 * OUTS, dtype=jnp.int32),
        ],
        [pltpu.HBM] * 8,
        [
            pltpu.SMEM((OUTS,), jnp.int32),
            pltpu.SMEM((OUTS,), jnp.int32),
            pltpu.SMEM((OUTS,), jnp.int32),
            pltpu.VMEM((7, panels_here), F32),
            pltpu.VMEM((RIGHT_SIDES, panels_here), BF16),
            pltpu.VMEM((RANK, panels_here), BF16),
            pltpu.VMEM((LEAVES, RANK, RANK), BF16),
            pltpu.VMEM((OUTS, RANK, RANK), BF16),
            coeff_work,
            pltpu.VMEM((2 * PEERS * NA, 128), F32),
            pltpu.SMEM((NA * PEERS,), jnp.int32),
            pltpu.SemaphoreType.DMA((11,)),
        ],
        [VM, VM, SM],
    )
    first_merge = call(
        first_merge_body, "first_merge", [merged_shape, shape(NA, LEAVES * ROWS, 2 * 128)], [VM]
    )
    next_merge = call(merge_body, "merge", [merged_shape], [VM] * 2)
    nearby = call(
        near_body, "nearby",
        [shape(RIGHT_SIDES, panels_here, dtype=F32), shape(LEAVES * ROWS, 128, dtype=F32)], [VM] * 8,
    )

    def together(*arrays):
        return lax.optimization_barrier(arrays)

    def couple(value, send, packet, choice, kernel):
        columns = slice(panels_here, panels_here + RANK)
        arrived = lax.all_to_all(send, ("b", "y"), 0, 0, tiled=True)
        other = swap(packet, "c", 1)
        two = jnp.concatenate([packet[:RIGHT_SIDES, columns], other[:RIGHT_SIDES, columns]], axis=1)
        four = swap(two, "x", 1)
        arrived, four = together(arrived, four)
        if choice is None:
            merged, choice = first_merge(arrived)
        else:
            merged = next_merge(arrived, choice)[0]
        merged, four = together(merged, four)
        received = lax.all_to_all(merged, "a", 0, 0, axis_index_groups=[ORDER], tiled=True)
        eight = swap(jnp.concatenate([two, four], axis=1), "x", 2)
        if kernel is None:
            kernel = call(
                kernel_body, "kernel", [shape(panels_here, 2 * panels_here)], [VM, VM, SM],
                [pltpu.VMEM((8, panels_here), F32)],
            )(panels, other, near_mask)[0]
        base, spread = nearby(value, other, kernel, two, four, eight, cluster_coupling, leaf_transfer)
        return received, base, spread, choice, kernel

    operands = (
        out_leaf, out_wide.reshape(OUTS), out_target, panels, density, source_basis, leaf_transfer, coupling
    )
    send, packet, place = first(*[pltpu.with_memory_space_constraint(array, pltpu.HBM) for array in operands])
    received, base, spread, choice, kernel = couple(density, send, packet, None, None)
    first_pass, send, packet = call(
        middle_body, "middle", [values, shape(PEERS, CHUNK, 128), shape(RIGHT_SIDES, packet_width)],
        [VM, VM, VM, VM, SM, VM, VM, VM], [coeff_work],
    )(received, spread, base, target_basis, place, source_basis, leaf_transfer, coupling)

    received, base, spread, choice, kernel = couple(first_pass, send, packet, choice, kernel)
    second_pass = call(last_body, "last", [values], [VM] * 4)(received, spread, base, target_basis)[0]
    return (first_pass, second_pass)


def solution(mesh):
    every = ("a", "b", "y", "x", "c")
    grid = Mesh(np.asarray(mesh.devices).reshape(NA, NB, NY, NX, NC), every)
    cols, rows = P(None, every), P(every)
    in_specs = (cols, cols, rows, cols, rows, rows, rows, rows, rows, rows, cols)
    return jax.shard_map(shards, mesh=grid, in_specs=in_specs, out_specs=(cols, cols), check_vma=False)
```

```python
import math

import jax
import jax.numpy as jnp
import numpy as np
from jax import lax
from jax.experimental import pallas as pl
from jax.experimental.pallas import tpu as pltpu
from jax.sharding import Mesh, PartitionSpec as P

LEAF_SIZE = 128
RANK = 64
RIGHT_SIDES = 32
LEAVES = 4
OUTS = 64
SMOOTHING = 0.0625
NA, NB, NY, NX, NC = 8, 2, 4, 4, 2
PEERS = NB * NY
SLOTS = 2 * NA
ROWS = 16
CHUNK = SLOTS * ROWS
IDS = 16
FIRST_PAIR = 5
ORDER = [(FIRST_PAIR + i) % NA for i in range(NA)]
PARTS = 3
F32, BF16 = jnp.float32, jnp.bfloat16
NT = (((1,), (1,)), ((), ()))


def call(body, name, out_shape, in_spaces, scratch=(), out_spaces=None):
    return pl.pallas_call(
        body,
        out_shape=out_shape,
        in_specs=[pl.BlockSpec(memory_space=space) for space in in_spaces],
        out_specs=[pl.BlockSpec(memory_space=space) for space in out_spaces or [pltpu.VMEM] * len(out_shape)],
        scratch_shapes=list(scratch),
        compiler_params=pltpu.CompilerParams(vmem_limit_bytes=32 * 1024 * 1024),
        name=name,
    )


VM, SM = pltpu.VMEM, pltpu.SMEM


def dot(a, b, dims=None):
    if dims is None:
        return jnp.dot(a, b, preferred_element_type=F32)
    return lax.dot_general(a, b, dims, preferred_element_type=F32)


def pack(block):
    return jnp.concatenate([block[:ROWS], block[ROWS:]], axis=1)


def leaf_cols(leaf):
    return slice(leaf * LEAF_SIZE, (leaf + 1) * LEAF_SIZE)


def split_parts(value):
    high = value.astype(BF16)
    rest = value - high.astype(F32)
    middle = rest.astype(BF16)
    return high, middle, (rest - middle.astype(F32)).astype(BF16)


def leaf_coeffs(value_ref, basis_ref, transfer_ref, swap_ref, coeff_ref):
    cluster = jnp.zeros((RIGHT_SIDES, RANK), F32)
    for leaf in range(LEAVES):
        coeff = dot(value_ref[:, leaf_cols(leaf)], basis_ref[:, leaf_cols(leaf)], NT).astype(BF16)
        coeff_ref[leaf * RIGHT_SIDES : (leaf + 1) * RIGHT_SIDES, :] = coeff
        cluster += dot(coeff, transfer_ref[leaf])
    swap_ref[:RIGHT_SIDES, : LEAVES * LEAF_SIZE] = value_ref[...]
    swap_ref[:RIGHT_SIDES, LEAVES * LEAF_SIZE :] = jnp.concatenate([cluster, jnp.zeros_like(cluster)], axis=1).astype(BF16)


def product(block, place_ref, coupling_ref, coeff_ref, send_ref):
    place = place_ref[block]
    peer = lax.shift_right_logical(place, 8)
    row = pl.multiple_of(jnp.bitwise_and(place, CHUNK - 1), ROWS)
    source = pl.multiple_of(place_ref[OUTS + block], RIGHT_SIDES)
    packed = pack(dot(coeff_ref[pl.ds(source, RIGHT_SIDES), :], coupling_ref[block])).astype(BF16)
    send_ref[peer, pl.ds(row, ROWS), :] = packed


def clear(send_ref):
    for peer in range(PEERS):
        send_ref[peer, :CHUNK, :] = jnp.zeros((CHUNK, 128), BF16)


def first_body(
    leaf_hbm, wide_hbm, target_hbm, panel_hbm, value_hbm, basis_hbm, transfer_hbm, coupling_hbm,
    send_ref, swap_ref, place_ref,
    leaf_ref, wide_ref, target_ref, panel_ref, value_ref, basis_ref, transfer_ref, coupling_ref,
    coeff_ref, row_ref, count_ref, sems,
):
    pairs = [
        (wide_hbm, wide_ref), (target_hbm, target_ref), (leaf_hbm, leaf_ref),
        (value_hbm, value_ref), (basis_hbm, basis_ref), (transfer_hbm, transfer_ref), (panel_hbm, panel_ref),
    ]
    parts = 4
    each = OUTS // parts
    for part in range(parts):
        span = pl.ds(part * each, each)
        pairs.append((coupling_hbm.at[span], coupling_ref.at[span]))
    copies = [pltpu.make_async_copy(source, place, sems.at[i]) for i, (source, place) in enumerate(pairs)]
    for copy in copies:
        copy.start()
    for wide in range(NA * PEERS):
        count_ref[wide] = 0
    clear(send_ref)
    for copy in copies[:3]:
        copy.wait()
    row_ref[...] = jnp.zeros((2 * PEERS * NA, 128), F32)
    for block in range(OUTS):
        wide = wide_ref[block]
        turn = count_ref[wide]
        count_ref[wide] = turn + 1
        peer = jnp.bitwise_and(wide, PEERS - 1)
        pair = lax.shift_right_logical(wide, 3)
        place_ref[block] = peer * CHUNK + (pair * 2 + turn) * ROWS
        place_ref[OUTS + block] = leaf_ref[block] * RIGHT_SIDES
        spot = turn * (PEERS * NA) + peer * NA + pair
        row_ref[pl.ds(spot, 1), :] = jnp.full((1, 128), target_ref[block] + 1, jnp.int32).astype(F32)
    early = jnp.bitwise_and(lax.broadcasted_iota(jnp.int32, (NA, 128), 1), 2 * ROWS - 1) < ROWS
    for peer in range(PEERS):
        turns = [row_ref[(turn * PEERS + peer) * NA : (turn * PEERS + peer + 1) * NA, :] for turn in range(2)]
        ids = jnp.where(early, turns[0], turns[1])
        send_ref[peer, CHUNK:, :] = jnp.concatenate([ids, ids], axis=0).astype(BF16)
    for copy in copies[3:7]:
        copy.wait()
    leaf_coeffs(value_ref, basis_ref, transfer_ref, swap_ref, coeff_ref)
    swap_ref[RIGHT_SIDES:, :] = jnp.zeros((PARTS * ROWS, LEAVES * LEAF_SIZE + 128), BF16)
    panel = jnp.concatenate([panel_ref[...], jnp.zeros((ROWS - 7, LEAVES * LEAF_SIZE), F32)], axis=0)
    for part, rows in enumerate(split_parts(panel)):
        start = RIGHT_SIDES + part * ROWS
        swap_ref[start : start + ROWS, : LEAVES * LEAF_SIZE] = rows
    for part in range(parts):
        copies[7 + part].wait()
        for block in range(part * each, (part + 1) * each):
            product(block, place_ref, coupling_ref, coeff_ref, send_ref)


def merge(recv_ref, choice_ref, out_ref):
    for place, pair in enumerate(ORDER):
        blocks = [recv_ref[src, pair * 2 * ROWS : (pair + 1) * 2 * ROWS, :] for src in range(PEERS)]
        out_ref[place] = dot(choice_ref[pair], jnp.concatenate(blocks, axis=0)).astype(BF16)


def first_merge_body(recv_ref, out_ref, choice_ref):
    group = lax.shift_right_logical(lax.broadcasted_iota(jnp.int32, (NA, 128), 1), 5)
    halves = []
    for half in range(2):
        ids = jnp.zeros((NA, 128), F32)
        for src in range(4):
            rows = recv_ref[half * 4 + src, CHUNK : CHUNK + IDS, :].astype(F32)[:NA]
            ids += jnp.where(group == src, rows, 0.0)
        halves.append(ids)
    ids = jnp.concatenate(halves, axis=1)
    dims = (LEAVES * ROWS, 2 * 128)
    row, lane = lax.broadcasted_iota(jnp.int32, dims, 0), lax.broadcasted_iota(jnp.int32, dims, 1)
    same = jnp.bitwise_and(row, ROWS - 1) == jnp.bitwise_and(lane, ROWS - 1)
    wanted = jnp.where(same, lax.shift_right_logical(row, 4) + 1, -1).astype(F32)
    for pair in range(NA):
        here = jnp.broadcast_to(ids[pair : pair + 1, :], dims)
        choice_ref[pair] = jnp.where(here == wanted, 1.0, 0.0).astype(BF16)
    merge(recv_ref, choice_ref, out_ref)


def merge_body(recv_ref, choice_ref, out_ref):
    merge(recv_ref, choice_ref, out_ref)


def kernel_body(own_ref, packet_ref, mask_ref, kernel_ref, other_ref):
    width = LEAVES * LEAF_SIZE
    start = RIGHT_SIDES
    high, middle, low = [
        packet_ref[start + part * ROWS : start + (part + 1) * ROWS, :width].astype(F32) for part in range(PARTS)
    ]
    other_ref[...] = (high + (middle + low))[:8]
    columns = jnp.transpose(
        jnp.concatenate([own_ref[0:3, :], jnp.zeros((5, LEAVES * LEAF_SIZE), F32)], axis=0)
    )
    for leaf in range(LEAVES):
        place = [columns[leaf_cols(leaf), axis : axis + 1] for axis in range(3)]
        for side, ref in enumerate((own_ref, other_ref)):
            for near in range(max(leaf - 1, 0), min(leaf + 2, LEAVES)):
                source = [ref[row : row + 1, leaf_cols(near)] for row in range(7)]
                offset = [place[axis] - source[axis] for axis in range(3)]
                squared = offset[0] * offset[0] + offset[1] * offset[1] + offset[2] * offset[2] + SMOOTHING
                along = offset[0] * source[3] + offset[1] * source[4] + offset[2] * source[5]
                inverse = lax.rsqrt(squared)
                kernel = (source[6] * (1.0 / (4.0 * math.pi))) * along * (inverse * inverse * inverse)
                keep = mask_ref[leaf, side * LEAVES + near] != 0
                first = side * LEAVES * LEAF_SIZE
                kernel_ref[leaf_cols(leaf), first + near * LEAF_SIZE : first + (near + 1) * LEAF_SIZE] = jnp.where(
                    keep, kernel, 0.0
                ).astype(BF16)


def near_body(value_ref, other_ref, kernel_ref, base_ref):
    width = LEAVES * LEAF_SIZE
    for leaf in range(LEAVES):
        low, high = max(leaf - 1, 0) * LEAF_SIZE, min(leaf + 2, LEAVES) * LEAF_SIZE
        near = dot(value_ref[:, low:high], kernel_ref[leaf_cols(leaf), low:high], NT)
        near += dot(other_ref[:RIGHT_SIDES, low:high], kernel_ref[leaf_cols(leaf), width + low : width + high], NT)
        base_ref[:, leaf_cols(leaf)] = near + 0.5 * value_ref[:, leaf_cols(leaf)].astype(F32)


def spread_body(two_ref, four_ref, eight_ref, rows_ref, transfer_ref, spread_ref):
    me = lax.axis_index("x") * NC + lax.axis_index("c")
    down = jnp.zeros((RIGHT_SIDES, RANK), F32)
    pairs = [two_ref[...], four_ref[...], eight_ref[:, :128], eight_ref[:, 128:]]
    for step, pair in enumerate(pairs):
        rows = [
            rows_ref[0, pl.ds(pl.multiple_of(jnp.bitwise_xor(me, 2 * step + turn) * RANK, RANK), RANK), :]
            for turn in range(2)
        ]
        down += dot(pair, jnp.concatenate(rows, axis=0))
    high = down.astype(BF16)
    low = (down - high.astype(F32)).astype(BF16)
    for leaf in range(LEAVES):
        spread = dot(high, transfer_ref[leaf], NT) + dot(low, transfer_ref[leaf], NT)
        spread_ref[leaf * ROWS : (leaf + 1) * ROWS, :] = pack(spread)


def finish(recv_ref, spread_ref, base_ref, target_ref, out_ref):
    field = spread_ref[...]
    for src in range(NA):
        field += recv_ref[src].astype(F32)
    field = field.astype(BF16)
    lower = lax.broadcasted_iota(jnp.int32, (ROWS, 128), 1) < RANK
    for leaf in range(LEAVES):
        block = field[leaf * ROWS : (leaf + 1) * ROWS, :].astype(F32)
        tall = jnp.concatenate([jnp.where(lower, block, 0.0), jnp.where(lower, 0.0, block)], axis=0).astype(BF16)
        basis = target_ref[:, leaf_cols(leaf)]
        far = dot(tall, jnp.concatenate([basis, basis], axis=0))
        out_ref[:, leaf_cols(leaf)] = (base_ref[:, leaf_cols(leaf)] + far).astype(BF16)


def middle_body(
    recv_ref, spread_ref, base_ref, target_ref, place_ref, basis_ref, transfer_ref, coupling_ref,
    out_ref, send_ref, swap_ref, coeff_ref,
):
    finish(recv_ref, spread_ref, base_ref, target_ref, out_ref)
    clear(send_ref)
    leaf_coeffs(out_ref, basis_ref, transfer_ref, swap_ref, coeff_ref)
    for block in range(OUTS):
        product(block, place_ref, coupling_ref, coeff_ref, send_ref)


def last_body(recv_ref, spread_ref, base_ref, target_ref, out_ref):
    finish(recv_ref, spread_ref, base_ref, target_ref, out_ref)


def shape(*dims, dtype=BF16):
    return jax.ShapeDtypeStruct(dims, dtype)


def shards(
    density, panels, near_mask, source_basis, leaf_transfer, cluster_coupling,
    out_leaf, out_wide, out_target, coupling, target_basis,
):
    panels_here = LEAVES * LEAF_SIZE
    values = shape(RIGHT_SIDES, panels_here)
    packet_width = panels_here + 128
    merged_shape = shape(NA, LEAVES * ROWS, 128)
    coeff_work = pltpu.VMEM((LEAVES * RIGHT_SIDES, RANK), BF16)

    def swap(block, axis, distance):
        count = lax.axis_size(axis)
        return lax.ppermute(block, axis, [(i, i ^ distance) for i in range(count)])

    first = call(
        first_body, "first",
        [
            shape(PEERS, CHUNK + IDS, 128), shape(RIGHT_SIDES + PARTS * ROWS, packet_width),
            shape(2 * OUTS, dtype=jnp.int32),
        ],
        [pltpu.HBM] * 8,
        [
            pltpu.SMEM((OUTS,), jnp.int32),
            pltpu.SMEM((OUTS,), jnp.int32),
            pltpu.SMEM((OUTS,), jnp.int32),
            pltpu.VMEM((7, panels_here), F32),
            pltpu.VMEM((RIGHT_SIDES, panels_here), BF16),
            pltpu.VMEM((RANK, panels_here), BF16),
            pltpu.VMEM((LEAVES, RANK, RANK), BF16),
            pltpu.VMEM((OUTS, RANK, RANK), BF16),
            coeff_work,
            pltpu.VMEM((2 * PEERS * NA, 128), F32),
            pltpu.SMEM((NA * PEERS,), jnp.int32),
            pltpu.SemaphoreType.DMA((11,)),
        ],
        [VM, VM, SM],
    )
    first_merge = call(
        first_merge_body, "first_merge", [merged_shape, shape(NA, LEAVES * ROWS, 2 * 128)], [VM]
    )
    next_merge = call(merge_body, "merge", [merged_shape], [VM] * 2)
    nearby = call(near_body, "nearby", [shape(RIGHT_SIDES, panels_here, dtype=F32)], [VM] * 3)
    spreading = call(spread_body, "spread", [shape(LEAVES * ROWS, 128, dtype=F32)], [VM] * 5)

    def together(*arrays):
        return lax.optimization_barrier(arrays)

    def couple(value, send, packet, choice, kernel):
        columns = slice(panels_here, panels_here + RANK)
        arrived = lax.all_to_all(send, ("b", "y"), 0, 0, tiled=True)
        other = swap(packet, "c", 1)
        two = jnp.concatenate([packet[:RIGHT_SIDES, columns], other[:RIGHT_SIDES, columns]], axis=1)
        four = swap(two, "x", 1)
        if kernel is None:
            kernel = call(
                kernel_body, "kernel", [shape(panels_here, 2 * panels_here)], [VM, VM, SM],
                [pltpu.VMEM((8, panels_here), F32)],
            )(panels, other, near_mask)[0]
        base = nearby(value, other, kernel)[0]
        arrived, four, base = together(arrived, four, base)
        if choice is None:
            merged, choice = first_merge(arrived)
        else:
            merged = next_merge(arrived, choice)[0]
        merged, four = together(merged, four)
        received = lax.all_to_all(merged, "a", 0, 0, axis_index_groups=[ORDER], tiled=True)
        eight = swap(jnp.concatenate([two, four], axis=1), "x", 2)
        spread = spreading(two, four, eight, cluster_coupling, leaf_transfer)[0]
        return received, base, spread, choice, kernel

    operands = (
        out_leaf, out_wide.reshape(OUTS), out_target, panels, density, source_basis, leaf_transfer, coupling
    )
    send, packet, place = first(*[pltpu.with_memory_space_constraint(array, pltpu.HBM) for array in operands])
    received, base, spread, choice, kernel = couple(density, send, packet, None, None)
    first_pass, send, packet = call(
        middle_body, "middle", [values, shape(PEERS, CHUNK, 128), shape(RIGHT_SIDES, packet_width)],
        [VM, VM, VM, VM, SM, VM, VM, VM], [coeff_work],
    )(received, spread, base, target_basis, place, source_basis, leaf_transfer, coupling)

    received, base, spread, choice, kernel = couple(first_pass, send, packet, choice, kernel)
    second_pass = call(last_body, "last", [values], [VM] * 4)(received, spread, base, target_basis)[0]
    return (first_pass, second_pass)


def solution(mesh):
    every = ("a", "b", "y", "x", "c")
    grid = Mesh(np.asarray(mesh.devices).reshape(NA, NB, NY, NX, NC), every)
    cols, rows = P(None, every), P(every)
    in_specs = (cols, cols, rows, cols, rows, rows, rows, rows, rows, rows, cols)
    return jax.shard_map(shards, mesh=grid, in_specs=in_specs, out_specs=(cols, cols), check_vma=False)
```

```python
import math

import jax
import jax.numpy as jnp
import numpy as np
from jax import lax
from jax.experimental import pallas as pl
from jax.experimental.pallas import tpu as pltpu
from jax.sharding import Mesh, PartitionSpec as P

LEAF_SIZE = 128
RANK = 64
RIGHT_SIDES = 32
LEAVES = 4
OUTS = 64
SMOOTHING = 0.0625
NA, NB, NY, NX, NC = 8, 2, 4, 4, 2
PEERS = NB * NY
SLOTS = 2 * NA
ROWS = 16
CHUNK = SLOTS * ROWS
IDS = 16
FIRST_PAIR = 5
ORDER = [(FIRST_PAIR + i) % NA for i in range(NA)]
PARTS = 3
F32, BF16 = jnp.float32, jnp.bfloat16
NT = (((1,), (1,)), ((), ()))


def call(body, name, out_shape, in_spaces, scratch=(), out_spaces=None):
    return pl.pallas_call(
        body,
        out_shape=out_shape,
        in_specs=[pl.BlockSpec(memory_space=space) for space in in_spaces],
        out_specs=[pl.BlockSpec(memory_space=space) for space in out_spaces or [pltpu.VMEM] * len(out_shape)],
        scratch_shapes=list(scratch),
        compiler_params=pltpu.CompilerParams(vmem_limit_bytes=32 * 1024 * 1024),
        name=name,
    )


VM, SM = pltpu.VMEM, pltpu.SMEM


def dot(a, b, dims=None):
    if dims is None:
        return jnp.dot(a, b, preferred_element_type=F32)
    return lax.dot_general(a, b, dims, preferred_element_type=F32)


def pack(block):
    return jnp.concatenate([block[:ROWS], block[ROWS:]], axis=1)


def leaf_cols(leaf):
    return slice(leaf * LEAF_SIZE, (leaf + 1) * LEAF_SIZE)


def split_parts(value):
    high = value.astype(BF16)
    rest = value - high.astype(F32)
    middle = rest.astype(BF16)
    return high, middle, (rest - middle.astype(F32)).astype(BF16)


def leaf_coeffs(value_ref, basis_ref, transfer_ref, swap_ref, coeff_ref):
    cluster = jnp.zeros((RIGHT_SIDES, RANK), F32)
    for leaf in range(LEAVES):
        coeff = dot(value_ref[:, leaf_cols(leaf)], basis_ref[:, leaf_cols(leaf)], NT).astype(BF16)
        coeff_ref[leaf * RIGHT_SIDES : (leaf + 1) * RIGHT_SIDES, :] = coeff
        cluster += dot(coeff, transfer_ref[leaf])
    swap_ref[:RIGHT_SIDES, : LEAVES * LEAF_SIZE] = value_ref[...]
    swap_ref[:RIGHT_SIDES, LEAVES * LEAF_SIZE :] = jnp.concatenate([cluster, jnp.zeros_like(cluster)], axis=1).astype(BF16)


def product(block, place_ref, coupling_ref, coeff_ref, send_ref):
    place = place_ref[block]
    peer = lax.shift_right_logical(place, 8)
    row = pl.multiple_of(jnp.bitwise_and(place, CHUNK - 1), ROWS)
    source = pl.multiple_of(place_ref[OUTS + block], RIGHT_SIDES)
    packed = pack(dot(coeff_ref[pl.ds(source, RIGHT_SIDES), :], coupling_ref[block])).astype(BF16)
    send_ref[peer, pl.ds(row, ROWS), :] = packed


def clear(send_ref):
    for peer in range(PEERS):
        send_ref[peer, :CHUNK, :] = jnp.zeros((CHUNK, 128), BF16)


def first_body(
    leaf_hbm, wide_hbm, target_hbm, panel_hbm, value_hbm, basis_hbm, transfer_hbm, coupling_hbm,
    send_ref, swap_ref, place_ref,
    leaf_ref, wide_ref, target_ref, panel_ref, value_ref, basis_ref, transfer_ref, coupling_ref,
    coeff_ref, row_ref, count_ref, sems,
):
    pairs = [
        (wide_hbm, wide_ref), (target_hbm, target_ref), (leaf_hbm, leaf_ref),
        (value_hbm, value_ref), (basis_hbm, basis_ref), (transfer_hbm, transfer_ref), (panel_hbm, panel_ref),
        (coupling_hbm, coupling_ref),
    ]
    copies = [pltpu.make_async_copy(source, place, sems.at[i]) for i, (source, place) in enumerate(pairs)]
    for copy in copies:
        copy.start()
    for wide in range(NA * PEERS):
        count_ref[wide] = 0
    clear(send_ref)
    for copy in copies[:3]:
        copy.wait()
    row_ref[...] = jnp.zeros((2 * PEERS * NA, 128), F32)
    for block in range(OUTS):
        wide = wide_ref[block]
        turn = count_ref[wide]
        count_ref[wide] = turn + 1
        peer = jnp.bitwise_and(wide, PEERS - 1)
        pair = lax.shift_right_logical(wide, 3)
        place_ref[block] = peer * CHUNK + (pair * 2 + turn) * ROWS
        place_ref[OUTS + block] = leaf_ref[block] * RIGHT_SIDES
        spot = turn * (PEERS * NA) + peer * NA + pair
        row_ref[pl.ds(spot, 1), :] = jnp.full((1, 128), target_ref[block] + 1, jnp.int32).astype(F32)
    early = jnp.bitwise_and(lax.broadcasted_iota(jnp.int32, (NA, 128), 1), 2 * ROWS - 1) < ROWS
    for peer in range(PEERS):
        turns = [row_ref[(turn * PEERS + peer) * NA : (turn * PEERS + peer + 1) * NA, :] for turn in range(2)]
        ids = jnp.where(early, turns[0], turns[1])
        send_ref[peer, CHUNK:, :] = jnp.concatenate([ids, ids], axis=0).astype(BF16)
    for copy in copies[3:7]:
        copy.wait()
    leaf_coeffs(value_ref, basis_ref, transfer_ref, swap_ref, coeff_ref)
    swap_ref[RIGHT_SIDES:, :] = jnp.zeros((PARTS * ROWS, LEAVES * LEAF_SIZE + 128), BF16)
    panel = jnp.concatenate([panel_ref[...], jnp.zeros((ROWS - 7, LEAVES * LEAF_SIZE), F32)], axis=0)
    for part, rows in enumerate(split_parts(panel)):
        start = RIGHT_SIDES + part * ROWS
        swap_ref[start : start + ROWS, : LEAVES * LEAF_SIZE] = rows
    copies[7].wait()
    for block in range(OUTS):
        product(block, place_ref, coupling_ref, coeff_ref, send_ref)


def merge(recv_ref, choice_ref, out_ref):
    for place, pair in enumerate(ORDER):
        blocks = [recv_ref[src, pair * 2 * ROWS : (pair + 1) * 2 * ROWS, :] for src in range(PEERS)]
        out_ref[place] = dot(choice_ref[pair], jnp.concatenate(blocks, axis=0)).astype(BF16)


def first_merge_body(recv_ref, out_ref, choice_ref):
    group = lax.shift_right_logical(lax.broadcasted_iota(jnp.int32, (NA, 128), 1), 5)
    halves = []
    for half in range(2):
        ids = jnp.zeros((NA, 128), F32)
        for src in range(4):
            rows = recv_ref[half * 4 + src, CHUNK : CHUNK + IDS, :].astype(F32)[:NA]
            ids += jnp.where(group == src, rows, 0.0)
        halves.append(ids)
    ids = jnp.concatenate(halves, axis=1)
    dims = (LEAVES * ROWS, 2 * 128)
    row, lane = lax.broadcasted_iota(jnp.int32, dims, 0), lax.broadcasted_iota(jnp.int32, dims, 1)
    same = jnp.bitwise_and(row, ROWS - 1) == jnp.bitwise_and(lane, ROWS - 1)
    wanted = jnp.where(same, lax.shift_right_logical(row, 4) + 1, -1).astype(F32)
    for pair in range(NA):
        here = jnp.broadcast_to(ids[pair : pair + 1, :], dims)
        choice_ref[pair] = jnp.where(here == wanted, 1.0, 0.0).astype(BF16)
    merge(recv_ref, choice_ref, out_ref)


def merge_body(recv_ref, choice_ref, out_ref):
    merge(recv_ref, choice_ref, out_ref)


def kernel_body(own_ref, packet_ref, mask_ref, kernel_ref, other_ref):
    width = LEAVES * LEAF_SIZE
    start = RIGHT_SIDES
    high, middle, low = [
        packet_ref[start + part * ROWS : start + (part + 1) * ROWS, :width].astype(F32) for part in range(PARTS)
    ]
    other_ref[...] = (high + (middle + low))[:8]
    columns = jnp.transpose(
        jnp.concatenate([own_ref[0:3, :], jnp.zeros((5, LEAVES * LEAF_SIZE), F32)], axis=0)
    )
    for leaf in range(LEAVES):
        place = [columns[leaf_cols(leaf), axis : axis + 1] for axis in range(3)]
        for side, ref in enumerate((own_ref, other_ref)):
            for near in range(max(leaf - 1, 0), min(leaf + 2, LEAVES)):
                source = [ref[row : row + 1, leaf_cols(near)] for row in range(7)]
                offset = [place[axis] - source[axis] for axis in range(3)]
                squared = offset[0] * offset[0] + offset[1] * offset[1] + offset[2] * offset[2] + SMOOTHING
                along = offset[0] * source[3] + offset[1] * source[4] + offset[2] * source[5]
                inverse = lax.rsqrt(squared)
                kernel = (source[6] * (1.0 / (4.0 * math.pi))) * along * (inverse * inverse * inverse)
                keep = mask_ref[leaf, side * LEAVES + near] != 0
                first = side * LEAVES * LEAF_SIZE
                kernel_ref[leaf_cols(leaf), first + near * LEAF_SIZE : first + (near + 1) * LEAF_SIZE] = jnp.where(
                    keep, kernel, 0.0
                ).astype(BF16)


def near_body(value_ref, other_ref, kernel_ref, base_ref):
    width = LEAVES * LEAF_SIZE
    for leaf in range(LEAVES):
        low, high = max(leaf - 1, 0) * LEAF_SIZE, min(leaf + 2, LEAVES) * LEAF_SIZE
        near = dot(value_ref[:, low:high], kernel_ref[leaf_cols(leaf), low:high], NT)
        near += dot(other_ref[:RIGHT_SIDES, low:high], kernel_ref[leaf_cols(leaf), width + low : width + high], NT)
        base_ref[:, leaf_cols(leaf)] = near + 0.5 * value_ref[:, leaf_cols(leaf)].astype(F32)


def spread_body(two_ref, four_ref, eight_ref, rows_ref, transfer_ref, spread_ref):
    me = lax.axis_index("x") * NC + lax.axis_index("c")
    down = jnp.zeros((RIGHT_SIDES, RANK), F32)
    pairs = [two_ref[...], four_ref[...], eight_ref[:, :128], eight_ref[:, 128:]]
    for step, pair in enumerate(pairs):
        rows = [
            rows_ref[0, pl.ds(pl.multiple_of(jnp.bitwise_xor(me, 2 * step + turn) * RANK, RANK), RANK), :]
            for turn in range(2)
        ]
        down += dot(pair, jnp.concatenate(rows, axis=0))
    high = down.astype(BF16)
    low = (down - high.astype(F32)).astype(BF16)
    for leaf in range(LEAVES):
        spread = dot(high, transfer_ref[leaf], NT) + dot(low, transfer_ref[leaf], NT)
        spread_ref[leaf * ROWS : (leaf + 1) * ROWS, :] = pack(spread)


def finish(recv_ref, spread_ref, base_ref, target_ref, out_ref):
    field = spread_ref[...]
    for src in range(NA):
        field += recv_ref[src].astype(F32)
    field = field.astype(BF16)
    lower = lax.broadcasted_iota(jnp.int32, (ROWS, 128), 1) < RANK
    for leaf in range(LEAVES):
        block = field[leaf * ROWS : (leaf + 1) * ROWS, :].astype(F32)
        tall = jnp.concatenate([jnp.where(lower, block, 0.0), jnp.where(lower, 0.0, block)], axis=0).astype(BF16)
        basis = target_ref[:, leaf_cols(leaf)]
        far = dot(tall, jnp.concatenate([basis, basis], axis=0))
        out_ref[:, leaf_cols(leaf)] = (base_ref[:, leaf_cols(leaf)] + far).astype(BF16)


def middle_body(
    recv_ref, spread_ref, base_ref, target_ref, place_ref, basis_ref, transfer_ref, coupling_ref,
    out_ref, send_ref, swap_ref, coeff_ref,
):
    finish(recv_ref, spread_ref, base_ref, target_ref, out_ref)
    clear(send_ref)
    leaf_coeffs(out_ref, basis_ref, transfer_ref, swap_ref, coeff_ref)
    for block in range(OUTS):
        product(block, place_ref, coupling_ref, coeff_ref, send_ref)


def last_body(recv_ref, spread_ref, base_ref, target_ref, out_ref):
    finish(recv_ref, spread_ref, base_ref, target_ref, out_ref)


def shape(*dims, dtype=BF16):
    return jax.ShapeDtypeStruct(dims, dtype)


def shards(
    density, panels, near_mask, source_basis, leaf_transfer, cluster_coupling,
    out_leaf, out_wide, out_target, coupling, target_basis,
):
    panels_here = LEAVES * LEAF_SIZE
    values = shape(RIGHT_SIDES, panels_here)
    packet_width = panels_here + 128
    merged_shape = shape(NA, LEAVES * ROWS, 128)
    coeff_work = pltpu.VMEM((LEAVES * RIGHT_SIDES, RANK), BF16)

    def swap(block, axis, distance):
        count = lax.axis_size(axis)
        return lax.ppermute(block, axis, [(i, i ^ distance) for i in range(count)])

    first = call(
        first_body, "first",
        [
            shape(PEERS, CHUNK + IDS, 128), shape(RIGHT_SIDES + PARTS * ROWS, packet_width),
            shape(2 * OUTS, dtype=jnp.int32),
        ],
        [pltpu.HBM] * 8,
        [
            pltpu.SMEM((OUTS,), jnp.int32),
            pltpu.SMEM((OUTS,), jnp.int32),
            pltpu.SMEM((OUTS,), jnp.int32),
            pltpu.VMEM((7, panels_here), F32),
            pltpu.VMEM((RIGHT_SIDES, panels_here), BF16),
            pltpu.VMEM((RANK, panels_here), BF16),
            pltpu.VMEM((LEAVES, RANK, RANK), BF16),
            pltpu.VMEM((OUTS, RANK, RANK), BF16),
            coeff_work,
            pltpu.VMEM((2 * PEERS * NA, 128), F32),
            pltpu.SMEM((NA * PEERS,), jnp.int32),
            pltpu.SemaphoreType.DMA((8,)),
        ],
        [VM, VM, SM],
    )
    first_merge = call(
        first_merge_body, "first_merge", [merged_shape, shape(NA, LEAVES * ROWS, 2 * 128)], [VM]
    )
    next_merge = call(merge_body, "merge", [merged_shape], [VM] * 2)
    nearby = call(near_body, "nearby", [shape(RIGHT_SIDES, panels_here, dtype=F32)], [VM] * 3)
    spreading = call(spread_body, "spread", [shape(LEAVES * ROWS, 128, dtype=F32)], [VM] * 5)

    def together(*arrays):
        return lax.optimization_barrier(arrays)

    def couple(value, send, packet, choice, kernel):
        columns = slice(panels_here, panels_here + RANK)
        arrived = lax.all_to_all(send, ("b", "y"), 0, 0, tiled=True)
        other = swap(packet, "c", 1)
        two = jnp.concatenate([packet[:RIGHT_SIDES, columns], other[:RIGHT_SIDES, columns]], axis=1)
        four = swap(two, "x", 1)
        if kernel is None:
            kernel = call(
                kernel_body, "kernel", [shape(panels_here, 2 * panels_here)], [VM, VM, SM],
                [pltpu.VMEM((8, panels_here), F32)],
            )(panels, other, near_mask)[0]
        base = nearby(value, other, kernel)[0]
        arrived, four, base = together(arrived, four, base)
        if choice is None:
            merged, choice = first_merge(arrived)
        else:
            merged = next_merge(arrived, choice)[0]
        merged, four = together(merged, four)
        received = lax.all_to_all(merged, "a", 0, 0, axis_index_groups=[ORDER], tiled=True)
        eight = swap(jnp.concatenate([two, four], axis=1), "x", 2)
        spread = spreading(two, four, eight, cluster_coupling, leaf_transfer)[0]
        return received, base, spread, choice, kernel

    operands = (
        out_leaf, out_wide.reshape(OUTS), out_target, panels, density, source_basis, leaf_transfer, coupling
    )
    send, packet, place = first(*[pltpu.with_memory_space_constraint(array, pltpu.HBM) for array in operands])
    received, base, spread, choice, kernel = couple(density, send, packet, None, None)
    first_pass, send, packet = call(
        middle_body, "middle", [values, shape(PEERS, CHUNK, 128), shape(RIGHT_SIDES, packet_width)],
        [VM, VM, VM, VM, SM, VM, VM, VM], [coeff_work],
    )(received, spread, base, target_basis, place, source_basis, leaf_transfer, coupling)

    received, base, spread, choice, kernel = couple(first_pass, send, packet, choice, kernel)
    second_pass = call(last_body, "last", [values], [VM] * 4)(received, spread, base, target_basis)[0]
    return (first_pass, second_pass)


def solution(mesh):
    every = ("a", "b", "y", "x", "c")
    grid = Mesh(np.asarray(mesh.devices).reshape(NA, NB, NY, NX, NC), every)
    cols, rows = P(None, every), P(every)
    in_specs = (cols, cols, rows, cols, rows, rows, rows, rows, rows, rows, cols)
    return jax.shard_map(shards, mesh=grid, in_specs=in_specs, out_specs=(cols, cols), check_vma=False)
```

```python
import math

import jax
import jax.numpy as jnp
import numpy as np
from jax import lax
from jax.experimental import pallas as pl
from jax.experimental.pallas import tpu as pltpu
from jax.sharding import Mesh, PartitionSpec as P

LEAF_SIZE = 128
RANK = 64
RIGHT_SIDES = 32
LEAVES = 4
OUTS = 64
SMOOTHING = 0.0625
NA, NB, NY, NX, NC = 8, 2, 4, 4, 2
PEERS = NB * NY
SLOTS = 2 * NA
ROWS = 16
CHUNK = SLOTS * ROWS
IDS = 16
FIRST_PAIR = 5
ORDER = [(FIRST_PAIR + i) % NA for i in range(NA)]
LATER_ORDER = [(4 + i) % NA for i in range(NA)]
PARTS = 3
F32, BF16 = jnp.float32, jnp.bfloat16
NT = (((1,), (1,)), ((), ()))


def call(body, name, out_shape, in_spaces, scratch=(), out_spaces=None):
    return pl.pallas_call(
        body,
        out_shape=out_shape,
        in_specs=[pl.BlockSpec(memory_space=space) for space in in_spaces],
        out_specs=[pl.BlockSpec(memory_space=space) for space in out_spaces or [pltpu.VMEM] * len(out_shape)],
        scratch_shapes=list(scratch),
        compiler_params=pltpu.CompilerParams(vmem_limit_bytes=32 * 1024 * 1024),
        name=name,
    )


VM, SM = pltpu.VMEM, pltpu.SMEM


def dot(a, b, dims=None):
    if dims is None:
        return jnp.dot(a, b, preferred_element_type=F32)
    return lax.dot_general(a, b, dims, preferred_element_type=F32)


def pack(block):
    return jnp.concatenate([block[:ROWS], block[ROWS:]], axis=1)


def leaf_cols(leaf):
    return slice(leaf * LEAF_SIZE, (leaf + 1) * LEAF_SIZE)


def split_parts(value):
    high = value.astype(BF16)
    rest = value - high.astype(F32)
    middle = rest.astype(BF16)
    return high, middle, (rest - middle.astype(F32)).astype(BF16)


def leaf_coeffs(value_ref, basis_ref, transfer_ref, swap_ref, coeff_ref):
    cluster = jnp.zeros((RIGHT_SIDES, RANK), F32)
    for leaf in range(LEAVES):
        coeff = dot(value_ref[:, leaf_cols(leaf)], basis_ref[:, leaf_cols(leaf)], NT).astype(BF16)
        coeff_ref[leaf * RIGHT_SIDES : (leaf + 1) * RIGHT_SIDES, :] = coeff
        cluster += dot(coeff, transfer_ref[leaf])
    swap_ref[:RIGHT_SIDES, : LEAVES * LEAF_SIZE] = value_ref[...]
    swap_ref[:RIGHT_SIDES, LEAVES * LEAF_SIZE :] = jnp.concatenate([cluster, jnp.zeros_like(cluster)], axis=1).astype(BF16)


def product(block, place_ref, coupling_ref, coeff_ref, send_ref):
    place = place_ref[block]
    peer = lax.shift_right_logical(place, 8)
    row = pl.multiple_of(jnp.bitwise_and(place, CHUNK - 1), ROWS)
    source = pl.multiple_of(place_ref[OUTS + block], RIGHT_SIDES)
    packed = pack(dot(coeff_ref[pl.ds(source, RIGHT_SIDES), :], coupling_ref[block])).astype(BF16)
    send_ref[peer, pl.ds(row, ROWS), :] = packed


def clear(send_ref):
    for peer in range(PEERS):
        send_ref[peer, :CHUNK, :] = jnp.zeros((CHUNK, 128), BF16)


def first_body(
    leaf_hbm, wide_hbm, target_hbm, panel_hbm, value_hbm, basis_hbm, transfer_hbm, coupling_hbm,
    send_ref, swap_ref, place_ref,
    leaf_ref, wide_ref, target_ref, panel_ref, value_ref, basis_ref, transfer_ref, coupling_ref,
    coeff_ref, row_ref, count_ref, sems,
):
    pairs = [
        (wide_hbm, wide_ref), (target_hbm, target_ref), (leaf_hbm, leaf_ref),
        (value_hbm, value_ref), (basis_hbm, basis_ref), (transfer_hbm, transfer_ref), (panel_hbm, panel_ref),
        (coupling_hbm, coupling_ref),
    ]
    copies = [pltpu.make_async_copy(source, place, sems.at[i]) for i, (source, place) in enumerate(pairs)]
    for copy in copies:
        copy.start()
    for wide in range(NA * PEERS):
        count_ref[wide] = 0
    clear(send_ref)
    for copy in copies[:3]:
        copy.wait()
    row_ref[...] = jnp.zeros((2 * PEERS * NA, 128), F32)
    for block in range(OUTS):
        wide = wide_ref[block]
        turn = count_ref[wide]
        count_ref[wide] = turn + 1
        peer = jnp.bitwise_and(wide, PEERS - 1)
        pair = lax.shift_right_logical(wide, 3)
        place_ref[block] = peer * CHUNK + (pair * 2 + turn) * ROWS
        place_ref[OUTS + block] = leaf_ref[block] * RIGHT_SIDES
        spot = turn * (PEERS * NA) + peer * NA + pair
        row_ref[pl.ds(spot, 1), :] = jnp.full((1, 128), target_ref[block] + 1, jnp.int32).astype(F32)
    early = jnp.bitwise_and(lax.broadcasted_iota(jnp.int32, (NA, 128), 1), 2 * ROWS - 1) < ROWS
    for peer in range(PEERS):
        turns = [row_ref[(turn * PEERS + peer) * NA : (turn * PEERS + peer + 1) * NA, :] for turn in range(2)]
        ids = jnp.where(early, turns[0], turns[1])
        send_ref[peer, CHUNK:, :] = jnp.concatenate([ids, ids], axis=0).astype(BF16)
    for copy in copies[3:7]:
        copy.wait()
    leaf_coeffs(value_ref, basis_ref, transfer_ref, swap_ref, coeff_ref)
    swap_ref[RIGHT_SIDES:, :] = jnp.zeros((PARTS * ROWS, LEAVES * LEAF_SIZE + 128), BF16)
    panel = jnp.concatenate([panel_ref[...], jnp.zeros((ROWS - 7, LEAVES * LEAF_SIZE), F32)], axis=0)
    for part, rows in enumerate(split_parts(panel)):
        start = RIGHT_SIDES + part * ROWS
        swap_ref[start : start + ROWS, : LEAVES * LEAF_SIZE] = rows
    copies[7].wait()
    for block in range(OUTS):
        product(block, place_ref, coupling_ref, coeff_ref, send_ref)


def merge(recv_ref, choice_ref, out_ref, order):
    for place, pair in enumerate(order):
        blocks = [recv_ref[src, pair * 2 * ROWS : (pair + 1) * 2 * ROWS, :] for src in range(PEERS)]
        out_ref[place] = dot(choice_ref[pair], jnp.concatenate(blocks, axis=0)).astype(BF16)


def first_merge_body(recv_ref, out_ref, choice_ref):
    group = lax.shift_right_logical(lax.broadcasted_iota(jnp.int32, (NA, 128), 1), 5)
    halves = []
    for half in range(2):
        ids = jnp.zeros((NA, 128), F32)
        for src in range(4):
            rows = recv_ref[half * 4 + src, CHUNK : CHUNK + IDS, :].astype(F32)[:NA]
            ids += jnp.where(group == src, rows, 0.0)
        halves.append(ids)
    ids = jnp.concatenate(halves, axis=1)
    dims = (LEAVES * ROWS, 2 * 128)
    row, lane = lax.broadcasted_iota(jnp.int32, dims, 0), lax.broadcasted_iota(jnp.int32, dims, 1)
    same = jnp.bitwise_and(row, ROWS - 1) == jnp.bitwise_and(lane, ROWS - 1)
    wanted = jnp.where(same, lax.shift_right_logical(row, 4) + 1, -1).astype(F32)
    for pair in range(NA):
        here = jnp.broadcast_to(ids[pair : pair + 1, :], dims)
        choice_ref[pair] = jnp.where(here == wanted, 1.0, 0.0).astype(BF16)
    merge(recv_ref, choice_ref, out_ref, ORDER)


def merge_body(recv_ref, choice_ref, out_ref):
    merge(recv_ref, choice_ref, out_ref, LATER_ORDER)


def kernel_body(own_ref, packet_ref, mask_ref, kernel_ref, other_ref):
    width = LEAVES * LEAF_SIZE
    start = RIGHT_SIDES
    high, middle, low = [
        packet_ref[start + part * ROWS : start + (part + 1) * ROWS, :width].astype(F32) for part in range(PARTS)
    ]
    other_ref[...] = (high + (middle + low))[:8]
    columns = jnp.transpose(
        jnp.concatenate([own_ref[0:3, :], jnp.zeros((5, LEAVES * LEAF_SIZE), F32)], axis=0)
    )
    for leaf in range(LEAVES):
        place = [columns[leaf_cols(leaf), axis : axis + 1] for axis in range(3)]
        for side, ref in enumerate((own_ref, other_ref)):
            for near in range(max(leaf - 1, 0), min(leaf + 2, LEAVES)):
                source = [ref[row : row + 1, leaf_cols(near)] for row in range(7)]
                offset = [place[axis] - source[axis] for axis in range(3)]
                squared = offset[0] * offset[0] + offset[1] * offset[1] + offset[2] * offset[2] + SMOOTHING
                along = offset[0] * source[3] + offset[1] * source[4] + offset[2] * source[5]
                inverse = lax.rsqrt(squared)
                kernel = (source[6] * (1.0 / (4.0 * math.pi))) * along * (inverse * inverse * inverse)
                keep = mask_ref[leaf, side * LEAVES + near] != 0
                first = side * LEAVES * LEAF_SIZE
                kernel_ref[leaf_cols(leaf), first + near * LEAF_SIZE : first + (near + 1) * LEAF_SIZE] = jnp.where(
                    keep, kernel, 0.0
                ).astype(BF16)


def near_body(value_ref, other_ref, kernel_ref, base_ref):
    width = LEAVES * LEAF_SIZE
    for leaf in range(LEAVES):
        low, high = max(leaf - 1, 0) * LEAF_SIZE, min(leaf + 2, LEAVES) * LEAF_SIZE
        near = dot(value_ref[:, low:high], kernel_ref[leaf_cols(leaf), low:high], NT)
        near += dot(other_ref[:RIGHT_SIDES, low:high], kernel_ref[leaf_cols(leaf), width + low : width + high], NT)
        base_ref[:, leaf_cols(leaf)] = near + 0.5 * value_ref[:, leaf_cols(leaf)].astype(F32)


def spread_body(two_ref, four_ref, eight_ref, rows_ref, transfer_ref, spread_ref):
    me = lax.axis_index("x") * NC + lax.axis_index("c")
    down = jnp.zeros((RIGHT_SIDES, RANK), F32)
    pairs = [two_ref[...], four_ref[...], eight_ref[:, :128], eight_ref[:, 128:]]
    for step, pair in zip((0, 1, 3, 2), pairs):
        rows = [
            rows_ref[0, pl.ds(pl.multiple_of(jnp.bitwise_xor(me, 2 * step + turn) * RANK, RANK), RANK), :]
            for turn in range(2)
        ]
        down += dot(pair, jnp.concatenate(rows, axis=0))
    high = down.astype(BF16)
    low = (down - high.astype(F32)).astype(BF16)
    for leaf in range(LEAVES):
        spread = dot(high, transfer_ref[leaf], NT) + dot(low, transfer_ref[leaf], NT)
        spread_ref[leaf * ROWS : (leaf + 1) * ROWS, :] = pack(spread)


def finish(recv_ref, spread_ref, base_ref, target_ref, out_ref):
    field = spread_ref[...]
    for src in range(NA):
        field += recv_ref[src].astype(F32)
    field = field.astype(BF16)
    lower = lax.broadcasted_iota(jnp.int32, (ROWS, 128), 1) < RANK
    for leaf in range(LEAVES):
        block = field[leaf * ROWS : (leaf + 1) * ROWS, :].astype(F32)
        tall = jnp.concatenate([jnp.where(lower, block, 0.0), jnp.where(lower, 0.0, block)], axis=0).astype(BF16)
        basis = target_ref[:, leaf_cols(leaf)]
        far = dot(tall, jnp.concatenate([basis, basis], axis=0))
        out_ref[:, leaf_cols(leaf)] = (base_ref[:, leaf_cols(leaf)] + far).astype(BF16)


def middle_body(
    recv_ref, spread_ref, base_ref, target_ref, place_ref, basis_ref, transfer_ref, coupling_ref,
    out_ref, send_ref, swap_ref, coeff_ref,
):
    finish(recv_ref, spread_ref, base_ref, target_ref, out_ref)
    clear(send_ref)
    leaf_coeffs(out_ref, basis_ref, transfer_ref, swap_ref, coeff_ref)
    for block in range(OUTS):
        product(block, place_ref, coupling_ref, coeff_ref, send_ref)


def last_body(recv_ref, spread_ref, base_ref, target_ref, out_ref):
    finish(recv_ref, spread_ref, base_ref, target_ref, out_ref)


def shape(*dims, dtype=BF16):
    return jax.ShapeDtypeStruct(dims, dtype)


def shards(
    density, panels, near_mask, source_basis, leaf_transfer, cluster_coupling,
    out_leaf, out_wide, out_target, coupling, target_basis,
):
    panels_here = LEAVES * LEAF_SIZE
    values = shape(RIGHT_SIDES, panels_here)
    packet_width = panels_here + 128
    merged_shape = shape(NA, LEAVES * ROWS, 128)
    coeff_work = pltpu.VMEM((LEAVES * RIGHT_SIDES, RANK), BF16)

    def swap(block, axis, distance):
        count = lax.axis_size(axis)
        return lax.ppermute(block, axis, [(i, i ^ distance) for i in range(count)])

    first = call(
        first_body, "first",
        [
            shape(PEERS, CHUNK + IDS, 128), shape(RIGHT_SIDES + PARTS * ROWS, packet_width),
            shape(2 * OUTS, dtype=jnp.int32),
        ],
        [pltpu.HBM] * 8,
        [
            pltpu.SMEM((OUTS,), jnp.int32),
            pltpu.SMEM((OUTS,), jnp.int32),
            pltpu.SMEM((OUTS,), jnp.int32),
            pltpu.VMEM((7, panels_here), F32),
            pltpu.VMEM((RIGHT_SIDES, panels_here), BF16),
            pltpu.VMEM((RANK, panels_here), BF16),
            pltpu.VMEM((LEAVES, RANK, RANK), BF16),
            pltpu.VMEM((OUTS, RANK, RANK), BF16),
            coeff_work,
            pltpu.VMEM((2 * PEERS * NA, 128), F32),
            pltpu.SMEM((NA * PEERS,), jnp.int32),
            pltpu.SemaphoreType.DMA((8,)),
        ],
        [VM, VM, SM],
    )
    first_merge = call(
        first_merge_body, "first_merge", [merged_shape, shape(NA, LEAVES * ROWS, 2 * 128)], [VM]
    )
    next_merge = call(merge_body, "merge", [merged_shape], [VM] * 2)
    nearby = call(near_body, "nearby", [shape(RIGHT_SIDES, panels_here, dtype=F32)], [VM] * 3)
    spreading = call(spread_body, "spread", [shape(LEAVES * ROWS, 128, dtype=F32)], [VM] * 5)

    def together(*arrays):
        return lax.optimization_barrier(arrays)

    def couple(value, send, packet, choice, kernel):
        columns = slice(panels_here, panels_here + RANK)
        arrived = lax.all_to_all(send, ("b", "y"), 0, 0, tiled=True)
        other = swap(packet, "c", 1)
        two = jnp.concatenate([packet[:RIGHT_SIDES, columns], other[:RIGHT_SIDES, columns]], axis=1)
        four = swap(two, "x", 1)
        if kernel is None:
            kernel = call(
                kernel_body, "kernel", [shape(panels_here, 2 * panels_here)], [VM, VM, SM],
                [pltpu.VMEM((8, panels_here), F32)],
            )(panels, other, near_mask)[0]
        base = nearby(value, other, kernel)[0]
        arrived, four, base = together(arrived, four, base)
        if choice is None:
            order = ORDER
            merged, choice = first_merge(arrived)
        else:
            order = LATER_ORDER
            merged = next_merge(arrived, choice)[0]
        merged, four = together(merged, four)
        received = lax.all_to_all(merged, "a", 0, 0, axis_index_groups=[order], tiled=True)
        eight = swap(jnp.concatenate([two, four], axis=1), "x", 3)
        spread = spreading(two, four, eight, cluster_coupling, leaf_transfer)[0]
        return received, base, spread, choice, kernel

    operands = (
        out_leaf, out_wide.reshape(OUTS), out_target, panels, density, source_basis, leaf_transfer, coupling
    )
    send, packet, place = first(*[pltpu.with_memory_space_constraint(array, pltpu.HBM) for array in operands])
    received, base, spread, choice, kernel = couple(density, send, packet, None, None)
    first_pass, send, packet = call(
        middle_body, "middle", [values, shape(PEERS, CHUNK, 128), shape(RIGHT_SIDES, packet_width)],
        [VM, VM, VM, VM, SM, VM, VM, VM], [coeff_work],
    )(received, spread, base, target_basis, place, source_basis, leaf_transfer, coupling)

    received, base, spread, choice, kernel = couple(first_pass, send, packet, choice, kernel)
    second_pass = call(last_body, "last", [values], [VM] * 4)(received, spread, base, target_basis)[0]
    return (first_pass, second_pass)


def solution(mesh):
    every = ("a", "b", "y", "x", "c")
    grid = Mesh(np.asarray(mesh.devices).reshape(NA, NB, NY, NX, NC), every)
    cols, rows = P(None, every), P(every)
    in_specs = (cols, cols, rows, cols, rows, rows, rows, rows, rows, rows, cols)
    return jax.shard_map(shards, mesh=grid, in_specs=in_specs, out_specs=(cols, cols), check_vma=False)
```

```python
import math

import jax
import jax.numpy as jnp
import numpy as np
from jax import lax
from jax.experimental import pallas as pl
from jax.experimental.pallas import tpu as pltpu
from jax.sharding import Mesh, PartitionSpec as P

LEAF_SIZE = 128
RANK = 64
RIGHT_SIDES = 32
LEAVES = 4
OUTS = 64
SMOOTHING = 0.0625
NA, NB, NY, NX, NC = 8, 2, 4, 4, 2
PEERS = NB * NY
SLOTS = 2 * NA
ROWS = 16
CHUNK = SLOTS * ROWS
IDS = 16
FIRST_PAIR = 5
ORDER = [(FIRST_PAIR + i) % NA for i in range(NA)]
LATER_ORDER = [(4 + i) % NA for i in range(NA)]
PARTS = 3
F32, BF16 = jnp.float32, jnp.bfloat16
NT = (((1,), (1,)), ((), ()))


def call(body, name, out_shape, in_spaces, scratch=(), out_spaces=None):
    return pl.pallas_call(
        body,
        out_shape=out_shape,
        in_specs=[pl.BlockSpec(memory_space=space) for space in in_spaces],
        out_specs=[pl.BlockSpec(memory_space=space) for space in out_spaces or [pltpu.VMEM] * len(out_shape)],
        scratch_shapes=list(scratch),
        compiler_params=pltpu.CompilerParams(vmem_limit_bytes=32 * 1024 * 1024),
        name=name,
    )


VM, SM = pltpu.VMEM, pltpu.SMEM


def dot(a, b, dims=None):
    if dims is None:
        return jnp.dot(a, b, preferred_element_type=F32)
    return lax.dot_general(a, b, dims, preferred_element_type=F32)


def pack(block):
    return jnp.concatenate([block[:ROWS], block[ROWS:]], axis=1)


def leaf_cols(leaf):
    return slice(leaf * LEAF_SIZE, (leaf + 1) * LEAF_SIZE)


def split_parts(value):
    high = value.astype(BF16)
    rest = value - high.astype(F32)
    middle = rest.astype(BF16)
    return high, middle, (rest - middle.astype(F32)).astype(BF16)


def leaf_coeffs(value_ref, basis_ref, transfer_ref, swap_ref, coeff_ref):
    cluster = jnp.zeros((RIGHT_SIDES, RANK), F32)
    for leaf in range(LEAVES):
        coeff = dot(value_ref[:, leaf_cols(leaf)], basis_ref[:, leaf_cols(leaf)], NT).astype(BF16)
        coeff_ref[leaf * RIGHT_SIDES : (leaf + 1) * RIGHT_SIDES, :] = coeff
        cluster += dot(coeff, transfer_ref[leaf])
    swap_ref[:RIGHT_SIDES, : LEAVES * LEAF_SIZE] = value_ref[...]
    swap_ref[:RIGHT_SIDES, LEAVES * LEAF_SIZE :] = jnp.concatenate([cluster, jnp.zeros_like(cluster)], axis=1).astype(BF16)


def product(block, place_ref, coupling_ref, coeff_ref, send_ref):
    place = place_ref[block]
    peer = lax.shift_right_logical(place, 8)
    row = pl.multiple_of(jnp.bitwise_and(place, CHUNK - 1), ROWS)
    source = pl.multiple_of(place_ref[OUTS + block], RIGHT_SIDES)
    packed = pack(dot(coeff_ref[pl.ds(source, RIGHT_SIDES), :], coupling_ref[block])).astype(BF16)
    send_ref[peer, pl.ds(row, ROWS), :] = packed


def clear(send_ref):
    for peer in range(PEERS):
        send_ref[peer, :CHUNK, :] = jnp.zeros((CHUNK, 128), BF16)


def first_body(
    leaf_hbm, wide_hbm, target_hbm, panel_hbm, value_hbm, basis_hbm, transfer_hbm, coupling_hbm,
    send_ref, swap_ref, place_ref,
    leaf_ref, wide_ref, target_ref, panel_ref, value_ref, basis_ref, transfer_ref, coupling_ref,
    coeff_ref, row_ref, count_ref, sems,
):
    pairs = [
        (wide_hbm, wide_ref), (target_hbm, target_ref), (leaf_hbm, leaf_ref),
        (value_hbm, value_ref), (basis_hbm, basis_ref), (transfer_hbm, transfer_ref), (panel_hbm, panel_ref),
        (coupling_hbm, coupling_ref),
    ]
    copies = [pltpu.make_async_copy(source, place, sems.at[i]) for i, (source, place) in enumerate(pairs)]
    for copy in copies:
        copy.start()
    for wide in range(NA * PEERS):
        count_ref[wide] = 0
    clear(send_ref)
    for copy in copies[:3]:
        copy.wait()
    row_ref[...] = jnp.zeros((2 * PEERS * NA, 128), F32)
    for block in range(OUTS):
        wide = wide_ref[block]
        turn = count_ref[wide]
        count_ref[wide] = turn + 1
        peer = jnp.bitwise_and(wide, PEERS - 1)
        pair = lax.shift_right_logical(wide, 3)
        place_ref[block] = peer * CHUNK + (pair * 2 + turn) * ROWS
        place_ref[OUTS + block] = leaf_ref[block] * RIGHT_SIDES
        spot = turn * (PEERS * NA) + peer * NA + pair
        row_ref[pl.ds(spot, 1), :] = jnp.full((1, 128), target_ref[block] + 1, jnp.int32).astype(F32)
    early = jnp.bitwise_and(lax.broadcasted_iota(jnp.int32, (NA, 128), 1), 2 * ROWS - 1) < ROWS
    for peer in range(PEERS):
        turns = [row_ref[(turn * PEERS + peer) * NA : (turn * PEERS + peer + 1) * NA, :] for turn in range(2)]
        ids = jnp.where(early, turns[0], turns[1])
        send_ref[peer, CHUNK:, :] = jnp.concatenate([ids, ids], axis=0).astype(BF16)
    for copy in copies[3:7]:
        copy.wait()
    leaf_coeffs(value_ref, basis_ref, transfer_ref, swap_ref, coeff_ref)
    swap_ref[RIGHT_SIDES:, :] = jnp.zeros((PARTS * ROWS, LEAVES * LEAF_SIZE + 128), BF16)
    panel = jnp.concatenate([panel_ref[...], jnp.zeros((ROWS - 7, LEAVES * LEAF_SIZE), F32)], axis=0)
    for part, rows in enumerate(split_parts(panel)):
        start = RIGHT_SIDES + part * ROWS
        swap_ref[start : start + ROWS, : LEAVES * LEAF_SIZE] = rows
    copies[7].wait()
    for block in range(OUTS):
        product(block, place_ref, coupling_ref, coeff_ref, send_ref)


def merge(recv_ref, choice_ref, out_ref, order):
    for place, pair in enumerate(order):
        blocks = [recv_ref[src, pair * 2 * ROWS : (pair + 1) * 2 * ROWS, :] for src in range(PEERS)]
        out_ref[place] = dot(choice_ref[pair], jnp.concatenate(blocks, axis=0)).astype(BF16)


def first_merge_body(recv_ref, out_ref, choice_ref):
    group = lax.shift_right_logical(lax.broadcasted_iota(jnp.int32, (NA, 128), 1), 5)
    halves = []
    for half in range(2):
        ids = jnp.zeros((NA, 128), F32)
        for src in range(4):
            rows = recv_ref[half * 4 + src, CHUNK : CHUNK + IDS, :].astype(F32)[:NA]
            ids += jnp.where(group == src, rows, 0.0)
        halves.append(ids)
    ids = jnp.concatenate(halves, axis=1)
    dims = (LEAVES * ROWS, 2 * 128)
    row, lane = lax.broadcasted_iota(jnp.int32, dims, 0), lax.broadcasted_iota(jnp.int32, dims, 1)
    same = jnp.bitwise_and(row, ROWS - 1) == jnp.bitwise_and(lane, ROWS - 1)
    wanted = jnp.where(same, lax.shift_right_logical(row, 4) + 1, -1).astype(F32)
    for pair in range(NA):
        here = jnp.broadcast_to(ids[pair : pair + 1, :], dims)
        choice_ref[pair] = jnp.where(here == wanted, 1.0, 0.0).astype(BF16)
    merge(recv_ref, choice_ref, out_ref, ORDER)


def merge_body(recv_ref, choice_ref, out_ref):
    merge(recv_ref, choice_ref, out_ref, LATER_ORDER)


def kernel_body(own_ref, packet_ref, mask_ref, kernel_ref, other_ref):
    width = LEAVES * LEAF_SIZE
    start = RIGHT_SIDES
    high, middle, low = [
        packet_ref[start + part * ROWS : start + (part + 1) * ROWS, :width].astype(F32) for part in range(PARTS)
    ]
    other_ref[...] = (high + (middle + low))[:8]
    columns = jnp.transpose(
        jnp.concatenate([own_ref[0:3, :], jnp.zeros((5, LEAVES * LEAF_SIZE), F32)], axis=0)
    )
    for leaf in range(LEAVES):
        place = [columns[leaf_cols(leaf), axis : axis + 1] for axis in range(3)]
        for side, ref in enumerate((own_ref, other_ref)):
            for near in range(max(leaf - 1, 0), min(leaf + 2, LEAVES)):
                source = [ref[row : row + 1, leaf_cols(near)] for row in range(7)]
                offset = [place[axis] - source[axis] for axis in range(3)]
                squared = offset[0] * offset[0] + offset[1] * offset[1] + offset[2] * offset[2] + SMOOTHING
                along = offset[0] * source[3] + offset[1] * source[4] + offset[2] * source[5]
                inverse = lax.rsqrt(squared)
                kernel = (source[6] * (1.0 / (4.0 * math.pi))) * along * (inverse * inverse * inverse)
                keep = mask_ref[leaf, side * LEAVES + near] != 0
                first = side * LEAVES * LEAF_SIZE
                kernel_ref[leaf_cols(leaf), first + near * LEAF_SIZE : first + (near + 1) * LEAF_SIZE] = jnp.where(
                    keep, kernel, 0.0
                ).astype(BF16)


def near_body(value_ref, other_ref, kernel_ref, base_ref):
    width = LEAVES * LEAF_SIZE
    for leaf in range(LEAVES):
        low, high = max(leaf - 1, 0) * LEAF_SIZE, min(leaf + 2, LEAVES) * LEAF_SIZE
        near = dot(value_ref[:, low:high], kernel_ref[leaf_cols(leaf), low:high], NT)
        near += dot(other_ref[:RIGHT_SIDES, low:high], kernel_ref[leaf_cols(leaf), width + low : width + high], NT)
        base_ref[:, leaf_cols(leaf)] = near + 0.5 * value_ref[:, leaf_cols(leaf)].astype(F32)


def spread_blocks(two_ref, four_ref, eight_ref, rows_ref, transfer_ref):
    me = lax.axis_index("x") * NC + lax.axis_index("c")
    down = jnp.zeros((RIGHT_SIDES, RANK), F32)
    pairs = [two_ref[...], four_ref[...], eight_ref[:, :128], eight_ref[:, 128:]]
    for step, pair in zip((0, 1, 3, 2), pairs):
        rows = [
            rows_ref[0, pl.ds(pl.multiple_of(jnp.bitwise_xor(me, 2 * step + turn) * RANK, RANK), RANK), :]
            for turn in range(2)
        ]
        down += dot(pair, jnp.concatenate(rows, axis=0))
    high = down.astype(BF16)
    low = (down - high.astype(F32)).astype(BF16)
    blocks = []
    for leaf in range(LEAVES):
        blocks.append(pack(dot(high, transfer_ref[leaf], NT) + dot(low, transfer_ref[leaf], NT)))
    return jnp.concatenate(blocks, axis=0)


def spread_body(two_ref, four_ref, eight_ref, rows_ref, transfer_ref, spread_ref):
    spread_ref[...] = spread_blocks(two_ref, four_ref, eight_ref, rows_ref, transfer_ref)


def finish(recv_ref, field, base_ref, target_ref, out_ref):
    for src in range(NA):
        field += recv_ref[src].astype(F32)
    field = field.astype(BF16)
    lower = lax.broadcasted_iota(jnp.int32, (ROWS, 128), 1) < RANK
    for leaf in range(LEAVES):
        block = field[leaf * ROWS : (leaf + 1) * ROWS, :].astype(F32)
        tall = jnp.concatenate([jnp.where(lower, block, 0.0), jnp.where(lower, 0.0, block)], axis=0).astype(BF16)
        basis = target_ref[:, leaf_cols(leaf)]
        far = dot(tall, jnp.concatenate([basis, basis], axis=0))
        out_ref[:, leaf_cols(leaf)] = (base_ref[:, leaf_cols(leaf)] + far).astype(BF16)


def middle_body(
    recv_ref, spread_ref, base_ref, target_ref, place_ref, basis_ref, transfer_ref, coupling_ref,
    out_ref, send_ref, swap_ref, coeff_ref,
):
    finish(recv_ref, spread_ref[...], base_ref, target_ref, out_ref)
    clear(send_ref)
    leaf_coeffs(out_ref, basis_ref, transfer_ref, swap_ref, coeff_ref)
    for block in range(OUTS):
        product(block, place_ref, coupling_ref, coeff_ref, send_ref)


def last_body(recv_ref, two_ref, four_ref, eight_ref, rows_ref, transfer_ref, base_ref, target_ref, out_ref):
    spread = spread_blocks(two_ref, four_ref, eight_ref, rows_ref, transfer_ref)
    finish(recv_ref, spread, base_ref, target_ref, out_ref)


def shape(*dims, dtype=BF16):
    return jax.ShapeDtypeStruct(dims, dtype)


def shards(
    density, panels, near_mask, source_basis, leaf_transfer, cluster_coupling,
    out_leaf, out_wide, out_target, coupling, target_basis,
):
    panels_here = LEAVES * LEAF_SIZE
    values = shape(RIGHT_SIDES, panels_here)
    packet_width = panels_here + 128
    merged_shape = shape(NA, LEAVES * ROWS, 128)
    coeff_work = pltpu.VMEM((LEAVES * RIGHT_SIDES, RANK), BF16)

    def swap(block, axis, distance):
        count = lax.axis_size(axis)
        return lax.ppermute(block, axis, [(i, i ^ distance) for i in range(count)])

    first = call(
        first_body, "first",
        [
            shape(PEERS, CHUNK + IDS, 128), shape(RIGHT_SIDES + PARTS * ROWS, packet_width),
            shape(2 * OUTS, dtype=jnp.int32),
        ],
        [pltpu.HBM] * 8,
        [
            pltpu.SMEM((OUTS,), jnp.int32),
            pltpu.SMEM((OUTS,), jnp.int32),
            pltpu.SMEM((OUTS,), jnp.int32),
            pltpu.VMEM((7, panels_here), F32),
            pltpu.VMEM((RIGHT_SIDES, panels_here), BF16),
            pltpu.VMEM((RANK, panels_here), BF16),
            pltpu.VMEM((LEAVES, RANK, RANK), BF16),
            pltpu.VMEM((OUTS, RANK, RANK), BF16),
            coeff_work,
            pltpu.VMEM((2 * PEERS * NA, 128), F32),
            pltpu.SMEM((NA * PEERS,), jnp.int32),
            pltpu.SemaphoreType.DMA((8,)),
        ],
        [VM, VM, SM],
    )
    first_merge = call(
        first_merge_body, "first_merge", [merged_shape, shape(NA, LEAVES * ROWS, 2 * 128)], [VM]
    )
    next_merge = call(merge_body, "merge", [merged_shape], [VM] * 2)
    nearby = call(near_body, "nearby", [shape(RIGHT_SIDES, panels_here, dtype=F32)], [VM] * 3)
    spreading = call(spread_body, "spread", [shape(LEAVES * ROWS, 128, dtype=F32)], [VM] * 5)

    def together(*arrays):
        return lax.optimization_barrier(arrays)

    def couple(value, send, packet, choice, kernel):
        columns = slice(panels_here, panels_here + RANK)
        arrived = lax.all_to_all(send, ("b", "y"), 0, 0, tiled=True)
        other = swap(packet, "c", 1)
        two = jnp.concatenate([packet[:RIGHT_SIDES, columns], other[:RIGHT_SIDES, columns]], axis=1)
        four = swap(two, "x", 1)
        if kernel is None:
            kernel = call(
                kernel_body, "kernel", [shape(panels_here, 2 * panels_here)], [VM, VM, SM],
                [pltpu.VMEM((8, panels_here), F32)],
            )(panels, other, near_mask)[0]
        base = nearby(value, other, kernel)[0]
        if choice is None:
            arrived, four, kernel = together(arrived, four, kernel)
        else:
            arrived, four, base = together(arrived, four, base)
        if choice is None:
            order = ORDER
            merged, choice = first_merge(arrived)
        else:
            order = LATER_ORDER
            merged = next_merge(arrived, choice)[0]
        merged, four = together(merged, four)
        received = lax.all_to_all(merged, "a", 0, 0, axis_index_groups=[order], tiled=True)
        eight = swap(jnp.concatenate([two, four], axis=1), "x", 3)
        return received, base, (two, four, eight, cluster_coupling, leaf_transfer), choice, kernel

    operands = (
        out_leaf, out_wide.reshape(OUTS), out_target, panels, density, source_basis, leaf_transfer, coupling
    )
    send, packet, place = first(*[pltpu.with_memory_space_constraint(array, pltpu.HBM) for array in operands])
    received, base, clusters, choice, kernel = couple(density, send, packet, None, None)
    first_pass, send, packet = call(
        middle_body, "middle", [values, shape(PEERS, CHUNK, 128), shape(RIGHT_SIDES, packet_width)],
        [VM, VM, VM, VM, SM, VM, VM, VM], [coeff_work],
    )(received, spreading(*clusters)[0], base, target_basis, place, source_basis, leaf_transfer, coupling)

    received, base, clusters, choice, kernel = couple(first_pass, send, packet, choice, kernel)
    second_pass = call(last_body, "last", [values], [VM] * 8)(received, *clusters, base, target_basis)[0]
    return (first_pass, second_pass)


def solution(mesh):
    every = ("a", "b", "y", "x", "c")
    grid = Mesh(np.asarray(mesh.devices).reshape(NA, NB, NY, NX, NC), every)
    cols, rows = P(None, every), P(every)
    in_specs = (cols, cols, rows, cols, rows, rows, rows, rows, rows, rows, cols)
    return jax.shard_map(shards, mesh=grid, in_specs=in_specs, out_specs=(cols, cols), check_vma=False)
```

```python
import math

import jax
import jax.numpy as jnp
import numpy as np
from jax import lax
from jax.experimental import pallas as pl
from jax.experimental.pallas import tpu as pltpu
from jax.sharding import Mesh, PartitionSpec as P

LEAF_SIZE = 128
RANK = 64
RIGHT_SIDES = 32
LEAVES = 4
OUTS = 64
SMOOTHING = 0.0625
NA, NB, NY, NX, NC = 8, 2, 4, 4, 2
PEERS = NB * NY
SLOTS = 2 * NA
ROWS = 16
CHUNK = SLOTS * ROWS
IDS = 16
FIRST_PAIR = 5
ORDER = [(FIRST_PAIR + i) % NA for i in range(NA)]
LATER_ORDER = [(4 + i) % NA for i in range(NA)]
PARTS = 3
F32, BF16 = jnp.float32, jnp.bfloat16
NT = (((1,), (1,)), ((), ()))


def call(body, name, out_shape, in_spaces, scratch=(), out_spaces=None):
    return pl.pallas_call(
        body,
        out_shape=out_shape,
        in_specs=[pl.BlockSpec(memory_space=space) for space in in_spaces],
        out_specs=[pl.BlockSpec(memory_space=space) for space in out_spaces or [pltpu.VMEM] * len(out_shape)],
        scratch_shapes=list(scratch),
        compiler_params=pltpu.CompilerParams(vmem_limit_bytes=32 * 1024 * 1024),
        name=name,
    )


VM, SM = pltpu.VMEM, pltpu.SMEM


def dot(a, b, dims=None):
    if dims is None:
        return jnp.dot(a, b, preferred_element_type=F32)
    return lax.dot_general(a, b, dims, preferred_element_type=F32)


def pack(block):
    return jnp.concatenate([block[:ROWS], block[ROWS:]], axis=1)


def leaf_cols(leaf):
    return slice(leaf * LEAF_SIZE, (leaf + 1) * LEAF_SIZE)


def split_parts(value):
    high = value.astype(BF16)
    rest = value - high.astype(F32)
    middle = rest.astype(BF16)
    return high, middle, (rest - middle.astype(F32)).astype(BF16)


def leaf_coeffs(value_ref, basis_ref, transfer_ref, swap_ref, coeff_ref):
    cluster = jnp.zeros((RIGHT_SIDES, RANK), F32)
    for leaf in range(LEAVES):
        coeff = dot(value_ref[:, leaf_cols(leaf)], basis_ref[:, leaf_cols(leaf)], NT).astype(BF16)
        coeff_ref[leaf * RIGHT_SIDES : (leaf + 1) * RIGHT_SIDES, :] = coeff
        cluster += dot(coeff, transfer_ref[leaf])
    swap_ref[:RIGHT_SIDES, : LEAVES * LEAF_SIZE] = value_ref[...]
    swap_ref[:RIGHT_SIDES, LEAVES * LEAF_SIZE :] = jnp.concatenate([cluster, jnp.zeros_like(cluster)], axis=1).astype(BF16)


def product(block, place_ref, coupling_ref, coeff_ref, send_ref):
    place = place_ref[block]
    peer = lax.shift_right_logical(place, 8)
    row = pl.multiple_of(jnp.bitwise_and(place, CHUNK - 1), ROWS)
    source = pl.multiple_of(place_ref[OUTS + block], RIGHT_SIDES)
    packed = pack(dot(coeff_ref[pl.ds(source, RIGHT_SIDES), :], coupling_ref[block])).astype(BF16)
    send_ref[peer, pl.ds(row, ROWS), :] = packed


def clear(send_ref):
    for peer in range(PEERS):
        send_ref[peer, :CHUNK, :] = jnp.zeros((CHUNK, 128), BF16)


def first_body(
    leaf_hbm, wide_hbm, target_hbm, panel_hbm, value_hbm, basis_hbm, transfer_hbm, coupling_hbm,
    send_ref, swap_ref, place_ref,
    leaf_ref, wide_ref, target_ref, panel_ref, value_ref, basis_ref, transfer_ref, coupling_ref,
    coeff_ref, row_ref, count_ref, sems,
):
    pairs = [
        (wide_hbm, wide_ref), (target_hbm, target_ref), (leaf_hbm, leaf_ref),
        (value_hbm, value_ref), (basis_hbm, basis_ref), (transfer_hbm, transfer_ref), (panel_hbm, panel_ref),
        (coupling_hbm, coupling_ref),
    ]
    copies = [pltpu.make_async_copy(source, place, sems.at[i]) for i, (source, place) in enumerate(pairs)]
    for copy in copies:
        copy.start()
    for wide in range(NA * PEERS):
        count_ref[wide] = 0
    clear(send_ref)
    for copy in copies[:3]:
        copy.wait()
    row_ref[...] = jnp.zeros((2 * PEERS * NA, 128), F32)
    for block in range(OUTS):
        wide = wide_ref[block]
        turn = count_ref[wide]
        count_ref[wide] = turn + 1
        peer = jnp.bitwise_and(wide, PEERS - 1)
        pair = lax.shift_right_logical(wide, 3)
        place_ref[block] = peer * CHUNK + (pair * 2 + turn) * ROWS
        place_ref[OUTS + block] = leaf_ref[block] * RIGHT_SIDES
        spot = turn * (PEERS * NA) + peer * NA + pair
        row_ref[pl.ds(spot, 1), :] = jnp.full((1, 128), target_ref[block] + 1, jnp.int32).astype(F32)
    early = jnp.bitwise_and(lax.broadcasted_iota(jnp.int32, (NA, 128), 1), 2 * ROWS - 1) < ROWS
    for peer in range(PEERS):
        turns = [row_ref[(turn * PEERS + peer) * NA : (turn * PEERS + peer + 1) * NA, :] for turn in range(2)]
        ids = jnp.where(early, turns[0], turns[1])
        send_ref[peer, CHUNK:, :] = jnp.concatenate([ids, ids], axis=0).astype(BF16)
    for copy in copies[3:7]:
        copy.wait()
    leaf_coeffs(value_ref, basis_ref, transfer_ref, swap_ref, coeff_ref)
    swap_ref[RIGHT_SIDES:, :] = jnp.zeros((PARTS * ROWS, LEAVES * LEAF_SIZE + 128), BF16)
    panel = jnp.concatenate([panel_ref[...], jnp.zeros((ROWS - 7, LEAVES * LEAF_SIZE), F32)], axis=0)
    for part, rows in enumerate(split_parts(panel)):
        start = RIGHT_SIDES + part * ROWS
        swap_ref[start : start + ROWS, : LEAVES * LEAF_SIZE] = rows
    copies[7].wait()
    for block in range(OUTS):
        product(block, place_ref, coupling_ref, coeff_ref, send_ref)


def merge(recv_ref, choice_ref, out_ref, order):
    for place, pair in enumerate(order):
        blocks = [recv_ref[src, pair * 2 * ROWS : (pair + 1) * 2 * ROWS, :] for src in range(PEERS)]
        out_ref[place] = dot(choice_ref[pair], jnp.concatenate(blocks, axis=0)).astype(BF16)


def first_merge_body(recv_ref, out_ref, choice_ref):
    group = lax.shift_right_logical(lax.broadcasted_iota(jnp.int32, (NA, 128), 1), 5)
    halves = []
    for half in range(2):
        ids = jnp.zeros((NA, 128), F32)
        for src in range(4):
            rows = recv_ref[half * 4 + src, CHUNK : CHUNK + IDS, :].astype(F32)[:NA]
            ids += jnp.where(group == src, rows, 0.0)
        halves.append(ids)
    ids = jnp.concatenate(halves, axis=1)
    dims = (LEAVES * ROWS, 2 * 128)
    row, lane = lax.broadcasted_iota(jnp.int32, dims, 0), lax.broadcasted_iota(jnp.int32, dims, 1)
    same = jnp.bitwise_and(row, ROWS - 1) == jnp.bitwise_and(lane, ROWS - 1)
    wanted = jnp.where(same, lax.shift_right_logical(row, 4) + 1, -1).astype(F32)
    for pair in range(NA):
        here = jnp.broadcast_to(ids[pair : pair + 1, :], dims)
        choice_ref[pair] = jnp.where(here == wanted, 1.0, 0.0).astype(BF16)
    merge(recv_ref, choice_ref, out_ref, ORDER)


def merge_body(recv_ref, choice_ref, out_ref):
    merge(recv_ref, choice_ref, out_ref, LATER_ORDER)


def kernel_body(own_ref, packet_ref, mask_ref, kernel_ref, other_ref):
    width = LEAVES * LEAF_SIZE
    start = RIGHT_SIDES
    high, middle, low = [
        packet_ref[start + part * ROWS : start + (part + 1) * ROWS, :width].astype(F32) for part in range(PARTS)
    ]
    other_ref[...] = (high + (middle + low))[:8]
    columns = jnp.transpose(
        jnp.concatenate([own_ref[0:3, :], jnp.zeros((5, LEAVES * LEAF_SIZE), F32)], axis=0)
    )
    for leaf in range(LEAVES):
        place = [columns[leaf_cols(leaf), axis : axis + 1] for axis in range(3)]
        for side, ref in enumerate((own_ref, other_ref)):
            for near in range(max(leaf - 1, 0), min(leaf + 2, LEAVES)):
                source = [ref[row : row + 1, leaf_cols(near)] for row in range(7)]
                offset = [place[axis] - source[axis] for axis in range(3)]
                squared = offset[0] * offset[0] + offset[1] * offset[1] + offset[2] * offset[2] + SMOOTHING
                along = offset[0] * source[3] + offset[1] * source[4] + offset[2] * source[5]
                inverse = lax.rsqrt(squared)
                kernel = (source[6] * (1.0 / (4.0 * math.pi))) * along * (inverse * inverse * inverse)
                keep = mask_ref[leaf, side * LEAVES + near] != 0
                first = side * LEAVES * LEAF_SIZE
                kernel_ref[leaf_cols(leaf), first + near * LEAF_SIZE : first + (near + 1) * LEAF_SIZE] = jnp.where(
                    keep, kernel, 0.0
                ).astype(BF16)


def near_body(value_ref, other_ref, kernel_ref, base_ref):
    width = LEAVES * LEAF_SIZE
    for leaf in range(LEAVES):
        low, high = max(leaf - 1, 0) * LEAF_SIZE, min(leaf + 2, LEAVES) * LEAF_SIZE
        near = dot(value_ref[:, low:high], kernel_ref[leaf_cols(leaf), low:high], NT)
        near += dot(other_ref[:RIGHT_SIDES, low:high], kernel_ref[leaf_cols(leaf), width + low : width + high], NT)
        base_ref[:, leaf_cols(leaf)] = near + 0.5 * value_ref[:, leaf_cols(leaf)].astype(F32)


def spread_blocks(two_ref, four_ref, eight_ref, rows_ref, transfer_ref):
    me = lax.axis_index("x") * NC + lax.axis_index("c")
    down = jnp.zeros((RIGHT_SIDES, RANK), F32)
    pairs = [two_ref[...], four_ref[...], eight_ref[:, :128], eight_ref[:, 128:]]
    for step, pair in zip((0, 1, 3, 2), pairs):
        rows = [
            rows_ref[0, pl.ds(pl.multiple_of(jnp.bitwise_xor(me, 2 * step + turn) * RANK, RANK), RANK), :]
            for turn in range(2)
        ]
        down += dot(pair, jnp.concatenate(rows, axis=0))
    high = down.astype(BF16)
    low = (down - high.astype(F32)).astype(BF16)
    blocks = []
    for leaf in range(LEAVES):
        blocks.append(pack(dot(high, transfer_ref[leaf], NT) + dot(low, transfer_ref[leaf], NT)))
    return jnp.concatenate(blocks, axis=0)


def spread_body(two_ref, four_ref, eight_ref, rows_ref, transfer_ref, spread_ref):
    spread_ref[...] = spread_blocks(two_ref, four_ref, eight_ref, rows_ref, transfer_ref)


def finish(recv_ref, field, base_ref, target_ref, out_ref):
    for src in range(NA):
        field += recv_ref[src].astype(F32)
    field = field.astype(BF16)
    lower = lax.broadcasted_iota(jnp.int32, (ROWS, 128), 1) < RANK
    for leaf in range(LEAVES):
        block = field[leaf * ROWS : (leaf + 1) * ROWS, :].astype(F32)
        tall = jnp.concatenate([jnp.where(lower, block, 0.0), jnp.where(lower, 0.0, block)], axis=0).astype(BF16)
        basis = target_ref[:, leaf_cols(leaf)]
        far = dot(tall, jnp.concatenate([basis, basis], axis=0))
        out_ref[:, leaf_cols(leaf)] = (base_ref[:, leaf_cols(leaf)] + far).astype(BF16)


def middle_body(
    recv_ref, two_ref, four_ref, eight_ref, rows_ref, base_ref, target_ref, place_ref, basis_ref, transfer_ref, coupling_ref,
    out_ref, send_ref, swap_ref, coeff_ref,
):
    spread = spread_blocks(two_ref, four_ref, eight_ref, rows_ref, transfer_ref)
    finish(recv_ref, spread, base_ref, target_ref, out_ref)
    clear(send_ref)
    leaf_coeffs(out_ref, basis_ref, transfer_ref, swap_ref, coeff_ref)
    for block in range(OUTS):
        product(block, place_ref, coupling_ref, coeff_ref, send_ref)


def last_body(recv_ref, two_ref, four_ref, eight_ref, rows_ref, transfer_ref, base_ref, target_ref, out_ref):
    spread = spread_blocks(two_ref, four_ref, eight_ref, rows_ref, transfer_ref)
    finish(recv_ref, spread, base_ref, target_ref, out_ref)


def shape(*dims, dtype=BF16):
    return jax.ShapeDtypeStruct(dims, dtype)


def shards(
    density, panels, near_mask, source_basis, leaf_transfer, cluster_coupling,
    out_leaf, out_wide, out_target, coupling, target_basis,
):
    panels_here = LEAVES * LEAF_SIZE
    values = shape(RIGHT_SIDES, panels_here)
    packet_width = panels_here + 128
    merged_shape = shape(NA, LEAVES * ROWS, 128)
    coeff_work = pltpu.VMEM((LEAVES * RIGHT_SIDES, RANK), BF16)

    def swap(block, axis, distance):
        count = lax.axis_size(axis)
        return lax.ppermute(block, axis, [(i, i ^ distance) for i in range(count)])

    first = call(
        first_body, "first",
        [
            shape(PEERS, CHUNK + IDS, 128), shape(RIGHT_SIDES + PARTS * ROWS, packet_width),
            shape(2 * OUTS, dtype=jnp.int32),
        ],
        [pltpu.HBM] * 8,
        [
            pltpu.SMEM((OUTS,), jnp.int32),
            pltpu.SMEM((OUTS,), jnp.int32),
            pltpu.SMEM((OUTS,), jnp.int32),
            pltpu.VMEM((7, panels_here), F32),
            pltpu.VMEM((RIGHT_SIDES, panels_here), BF16),
            pltpu.VMEM((RANK, panels_here), BF16),
            pltpu.VMEM((LEAVES, RANK, RANK), BF16),
            pltpu.VMEM((OUTS, RANK, RANK), BF16),
            coeff_work,
            pltpu.VMEM((2 * PEERS * NA, 128), F32),
            pltpu.SMEM((NA * PEERS,), jnp.int32),
            pltpu.SemaphoreType.DMA((8,)),
        ],
        [VM, VM, SM],
    )
    first_merge = call(
        first_merge_body, "first_merge", [merged_shape, shape(NA, LEAVES * ROWS, 2 * 128)], [VM]
    )
    next_merge = call(merge_body, "merge", [merged_shape], [VM] * 2)
    nearby = call(near_body, "nearby", [shape(RIGHT_SIDES, panels_here, dtype=F32)], [VM] * 3)
    spreading = call(spread_body, "spread", [shape(LEAVES * ROWS, 128, dtype=F32)], [VM] * 5)

    def together(*arrays):
        return lax.optimization_barrier(arrays)

    def couple(value, send, packet, choice, kernel):
        columns = slice(panels_here, panels_here + RANK)
        arrived = lax.all_to_all(send, ("b", "y"), 0, 0, tiled=True)
        other = swap(packet, "c", 1)
        two = jnp.concatenate([packet[:RIGHT_SIDES, columns], other[:RIGHT_SIDES, columns]], axis=1)
        four = swap(two, "x", 1)
        if kernel is None:
            kernel = call(
                kernel_body, "kernel", [shape(panels_here, 2 * panels_here)], [VM, VM, SM],
                [pltpu.VMEM((8, panels_here), F32)],
            )(panels, other, near_mask)[0]
        base = nearby(value, other, kernel)[0]
        if choice is None:
            arrived, four, kernel = together(arrived, four, kernel)
        else:
            arrived, four, base = together(arrived, four, base)
        if choice is None:
            order = ORDER
            merged, choice = first_merge(arrived)
        else:
            order = LATER_ORDER
            merged = next_merge(arrived, choice)[0]
        merged, four = together(merged, four)
        received = lax.all_to_all(merged, "a", 0, 0, axis_index_groups=[order], tiled=True)
        eight = swap(jnp.concatenate([two, four], axis=1), "x", 3)
        return received, base, (two, four, eight, cluster_coupling, leaf_transfer), choice, kernel

    operands = (
        out_leaf, out_wide.reshape(OUTS), out_target, panels, density, source_basis, leaf_transfer, coupling
    )
    send, packet, place = first(*[pltpu.with_memory_space_constraint(array, pltpu.HBM) for array in operands])
    received, base, clusters, choice, kernel = couple(density, send, packet, None, None)
    first_pass, send, packet = call(
        middle_body, "middle", [values, shape(PEERS, CHUNK, 128), shape(RIGHT_SIDES, packet_width)],
        [VM] * 7 + [SM] + [VM] * 3, [coeff_work],
    )(received, *clusters[:4], base, target_basis, place, source_basis, leaf_transfer, coupling)

    received, base, clusters, choice, kernel = couple(first_pass, send, packet, choice, kernel)
    second_pass = call(last_body, "last", [values], [VM] * 8)(received, *clusters, base, target_basis)[0]
    return (first_pass, second_pass)


def solution(mesh):
    every = ("a", "b", "y", "x", "c")
    grid = Mesh(np.asarray(mesh.devices).reshape(NA, NB, NY, NX, NC), every)
    cols, rows = P(None, every), P(every)
    in_specs = (cols, cols, rows, cols, rows, rows, rows, rows, rows, rows, cols)
    return jax.shard_map(shards, mesh=grid, in_specs=in_specs, out_specs=(cols, cols), check_vma=False)
```

```python
import math

import jax
import jax.numpy as jnp
import numpy as np
from jax import lax
from jax.experimental import pallas as pl
from jax.experimental.pallas import tpu as pltpu
from jax.sharding import Mesh, PartitionSpec as P

LEAF_SIZE = 128
RANK = 64
RIGHT_SIDES = 32
LEAVES = 4
OUTS = 64
SMOOTHING = 0.0625
NA, NB, NY, NX, NC = 8, 2, 4, 4, 2
PEERS = NB * NY
SLOTS = 2 * NA
ROWS = 16
CHUNK = SLOTS * ROWS
IDS = 16
FIRST_PAIR = 5
ORDER = [(FIRST_PAIR + i) % NA for i in range(NA)]
LATER_ORDER = [(4 + i) % NA for i in range(NA)]
PARTS = 3
F32, BF16 = jnp.float32, jnp.bfloat16
NT = (((1,), (1,)), ((), ()))


def call(body, name, out_shape, in_spaces, scratch=(), out_spaces=None):
    return pl.pallas_call(
        body,
        out_shape=out_shape,
        in_specs=[pl.BlockSpec(memory_space=space) for space in in_spaces],
        out_specs=[pl.BlockSpec(memory_space=space) for space in out_spaces or [pltpu.VMEM] * len(out_shape)],
        scratch_shapes=list(scratch),
        compiler_params=pltpu.CompilerParams(vmem_limit_bytes=32 * 1024 * 1024),
        name=name,
    )


VM, SM = pltpu.VMEM, pltpu.SMEM


def dot(a, b, dims=None):
    if dims is None:
        return jnp.dot(a, b, preferred_element_type=F32)
    return lax.dot_general(a, b, dims, preferred_element_type=F32)


def pack(block):
    return jnp.concatenate([block[:ROWS], block[ROWS:]], axis=1)


def leaf_cols(leaf):
    return slice(leaf * LEAF_SIZE, (leaf + 1) * LEAF_SIZE)


def split_parts(value):
    high = value.astype(BF16)
    rest = value - high.astype(F32)
    middle = rest.astype(BF16)
    return high, middle, (rest - middle.astype(F32)).astype(BF16)


def leaf_coeffs(value_ref, basis_ref, transfer_ref, swap_ref, coeff_ref):
    cluster = jnp.zeros((RIGHT_SIDES, RANK), F32)
    for leaf in range(LEAVES):
        coeff = dot(value_ref[:, leaf_cols(leaf)], basis_ref[:, leaf_cols(leaf)], NT).astype(BF16)
        coeff_ref[leaf * RIGHT_SIDES : (leaf + 1) * RIGHT_SIDES, :] = coeff
        cluster += dot(coeff, transfer_ref[leaf])
    swap_ref[:RIGHT_SIDES, : LEAVES * LEAF_SIZE] = value_ref[...]
    swap_ref[:RIGHT_SIDES, LEAVES * LEAF_SIZE :] = jnp.concatenate([cluster, jnp.zeros_like(cluster)], axis=1).astype(BF16)


def product(block, place_ref, coupling_ref, coeff_ref, send_ref):
    place = place_ref[block]
    peer = lax.shift_right_logical(place, 8)
    row = pl.multiple_of(jnp.bitwise_and(place, CHUNK - 1), ROWS)
    source = pl.multiple_of(place_ref[OUTS + block], RIGHT_SIDES)
    packed = pack(dot(coeff_ref[pl.ds(source, RIGHT_SIDES), :], coupling_ref[block])).astype(BF16)
    send_ref[peer, pl.ds(row, ROWS), :] = packed


def clear(send_ref):
    for peer in range(PEERS):
        send_ref[peer, :CHUNK, :] = jnp.zeros((CHUNK, 128), BF16)


def first_body(
    leaf_hbm, wide_hbm, target_hbm, panel_hbm, value_hbm, basis_hbm, transfer_hbm, coupling_hbm,
    send_ref, swap_ref, place_ref,
    leaf_ref, wide_ref, target_ref, panel_ref, value_ref, basis_ref, transfer_ref, coupling_ref,
    coeff_ref, row_ref, count_ref, sems,
):
    pairs = [
        (wide_hbm, wide_ref), (target_hbm, target_ref), (leaf_hbm, leaf_ref),
        (value_hbm, value_ref), (basis_hbm, basis_ref), (transfer_hbm, transfer_ref), (panel_hbm, panel_ref),
        (coupling_hbm, coupling_ref),
    ]
    copies = [pltpu.make_async_copy(source, place, sems.at[i]) for i, (source, place) in enumerate(pairs)]
    for copy in copies:
        copy.start()
    for wide in range(NA * PEERS):
        count_ref[wide] = 0
    clear(send_ref)
    swap_ref[RIGHT_SIDES:, LEAVES * LEAF_SIZE :] = jnp.zeros((PARTS * ROWS, 128), BF16)
    for copy in copies[:3]:
        copy.wait()
    row_ref[...] = jnp.zeros((2 * PEERS * NA, 128), F32)
    for block in range(OUTS):
        wide = wide_ref[block]
        turn = count_ref[wide]
        count_ref[wide] = turn + 1
        peer = jnp.bitwise_and(wide, PEERS - 1)
        pair = lax.shift_right_logical(wide, 3)
        place_ref[block] = peer * CHUNK + (pair * 2 + turn) * ROWS
        place_ref[OUTS + block] = leaf_ref[block] * RIGHT_SIDES
        spot = turn * (PEERS * NA) + peer * NA + pair
        row_ref[pl.ds(spot, 1), :] = jnp.full((1, 128), target_ref[block] + 1, jnp.int32).astype(F32)
    early = jnp.bitwise_and(lax.broadcasted_iota(jnp.int32, (NA, 128), 1), 2 * ROWS - 1) < ROWS
    for peer in range(PEERS):
        turns = [row_ref[(turn * PEERS + peer) * NA : (turn * PEERS + peer + 1) * NA, :] for turn in range(2)]
        ids = jnp.where(early, turns[0], turns[1])
        send_ref[peer, CHUNK:, :] = jnp.concatenate([ids, ids], axis=0).astype(BF16)
    for copy in copies[3:7]:
        copy.wait()
    leaf_coeffs(value_ref, basis_ref, transfer_ref, swap_ref, coeff_ref)
    panel = jnp.concatenate([panel_ref[...], jnp.zeros((ROWS - 7, LEAVES * LEAF_SIZE), F32)], axis=0)
    for part, rows in enumerate(split_parts(panel)):
        start = RIGHT_SIDES + part * ROWS
        swap_ref[start : start + ROWS, : LEAVES * LEAF_SIZE] = rows
    copies[7].wait()
    for block in range(OUTS):
        product(block, place_ref, coupling_ref, coeff_ref, send_ref)


def merge(recv_ref, choice_ref, out_ref, order):
    for place, pair in enumerate(order):
        blocks = [recv_ref[src, pair * 2 * ROWS : (pair + 1) * 2 * ROWS, :] for src in range(PEERS)]
        out_ref[place] = dot(choice_ref[pair], jnp.concatenate(blocks, axis=0)).astype(BF16)


def first_merge_body(recv_ref, out_ref, choice_ref):
    group = lax.shift_right_logical(lax.broadcasted_iota(jnp.int32, (NA, 128), 1), 5)
    halves = []
    for half in range(2):
        ids = jnp.zeros((NA, 128), F32)
        for src in range(4):
            rows = recv_ref[half * 4 + src, CHUNK : CHUNK + IDS, :].astype(F32)[:NA]
            ids += jnp.where(group == src, rows, 0.0)
        halves.append(ids)
    ids = jnp.concatenate(halves, axis=1)
    dims = (LEAVES * ROWS, 2 * 128)
    row, lane = lax.broadcasted_iota(jnp.int32, dims, 0), lax.broadcasted_iota(jnp.int32, dims, 1)
    same = jnp.bitwise_and(row, ROWS - 1) == jnp.bitwise_and(lane, ROWS - 1)
    wanted = jnp.where(same, lax.shift_right_logical(row, 4) + 1, -1).astype(F32)
    for pair in range(NA):
        here = jnp.broadcast_to(ids[pair : pair + 1, :], dims)
        choice_ref[pair] = jnp.where(here == wanted, 1.0, 0.0).astype(BF16)
    merge(recv_ref, choice_ref, out_ref, ORDER)


def merge_body(recv_ref, choice_ref, out_ref):
    merge(recv_ref, choice_ref, out_ref, LATER_ORDER)


def kernel_body(own_ref, packet_ref, mask_ref, kernel_ref, other_ref):
    width = LEAVES * LEAF_SIZE
    start = RIGHT_SIDES
    high, middle, low = [
        packet_ref[start + part * ROWS : start + (part + 1) * ROWS, :width].astype(F32) for part in range(PARTS)
    ]
    other_ref[...] = (high + (middle + low))[:8]
    columns = jnp.transpose(
        jnp.concatenate([own_ref[0:3, :], jnp.zeros((5, LEAVES * LEAF_SIZE), F32)], axis=0)
    )
    for leaf in range(LEAVES):
        place = [columns[leaf_cols(leaf), axis : axis + 1] for axis in range(3)]
        for side, ref in enumerate((own_ref, other_ref)):
            for near in range(max(leaf - 1, 0), min(leaf + 2, LEAVES)):
                source = [ref[row : row + 1, leaf_cols(near)] for row in range(7)]
                offset = [place[axis] - source[axis] for axis in range(3)]
                squared = offset[0] * offset[0] + offset[1] * offset[1] + offset[2] * offset[2] + SMOOTHING
                along = offset[0] * source[3] + offset[1] * source[4] + offset[2] * source[5]
                inverse = lax.rsqrt(squared)
                kernel = (source[6] * (1.0 / (4.0 * math.pi))) * along * (inverse * inverse * inverse)
                keep = mask_ref[leaf, side * LEAVES + near] != 0
                first = side * LEAVES * LEAF_SIZE
                kernel_ref[leaf_cols(leaf), first + near * LEAF_SIZE : first + (near + 1) * LEAF_SIZE] = jnp.where(
                    keep, kernel, 0.0
                ).astype(BF16)


def near_body(value_ref, other_ref, kernel_ref, base_ref):
    width = LEAVES * LEAF_SIZE
    for leaf in range(LEAVES):
        low, high = max(leaf - 1, 0) * LEAF_SIZE, min(leaf + 2, LEAVES) * LEAF_SIZE
        near = dot(value_ref[:, low:high], kernel_ref[leaf_cols(leaf), low:high], NT)
        near += dot(other_ref[:RIGHT_SIDES, low:high], kernel_ref[leaf_cols(leaf), width + low : width + high], NT)
        base_ref[:, leaf_cols(leaf)] = near + 0.5 * value_ref[:, leaf_cols(leaf)].astype(F32)


def spread_blocks(two_ref, four_ref, eight_ref, rows_ref, transfer_ref):
    me = lax.axis_index("x") * NC + lax.axis_index("c")
    down = jnp.zeros((RIGHT_SIDES, RANK), F32)
    pairs = [two_ref[...], four_ref[...], eight_ref[:, :128], eight_ref[:, 128:]]
    for step, pair in zip((0, 1, 3, 2), pairs):
        rows = [
            rows_ref[0, pl.ds(pl.multiple_of(jnp.bitwise_xor(me, 2 * step + turn) * RANK, RANK), RANK), :]
            for turn in range(2)
        ]
        down += dot(pair, jnp.concatenate(rows, axis=0))
    high = down.astype(BF16)
    low = (down - high.astype(F32)).astype(BF16)
    blocks = []
    for leaf in range(LEAVES):
        blocks.append(pack(dot(high, transfer_ref[leaf], NT) + dot(low, transfer_ref[leaf], NT)))
    return jnp.concatenate(blocks, axis=0)


def spread_body(two_ref, four_ref, eight_ref, rows_ref, transfer_ref, spread_ref):
    spread_ref[...] = spread_blocks(two_ref, four_ref, eight_ref, rows_ref, transfer_ref)


def finish(recv_ref, field, base_ref, target_ref, out_ref):
    for src in range(NA):
        field += recv_ref[src].astype(F32)
    field = field.astype(BF16)
    lower = lax.broadcasted_iota(jnp.int32, (ROWS, 128), 1) < RANK
    for leaf in range(LEAVES):
        block = field[leaf * ROWS : (leaf + 1) * ROWS, :].astype(F32)
        tall = jnp.concatenate([jnp.where(lower, block, 0.0), jnp.where(lower, 0.0, block)], axis=0).astype(BF16)
        basis = target_ref[:, leaf_cols(leaf)]
        far = dot(tall, jnp.concatenate([basis, basis], axis=0))
        out_ref[:, leaf_cols(leaf)] = (base_ref[:, leaf_cols(leaf)] + far).astype(BF16)


def middle_body(
    recv_ref, two_ref, four_ref, eight_ref, rows_ref, base_ref, target_ref, place_ref, basis_ref, transfer_ref, coupling_ref,
    out_ref, send_ref, swap_ref, coeff_ref,
):
    spread = spread_blocks(two_ref, four_ref, eight_ref, rows_ref, transfer_ref)
    finish(recv_ref, spread, base_ref, target_ref, out_ref)
    clear(send_ref)
    leaf_coeffs(out_ref, basis_ref, transfer_ref, swap_ref, coeff_ref)
    for block in range(OUTS):
        product(block, place_ref, coupling_ref, coeff_ref, send_ref)


def last_body(recv_ref, two_ref, four_ref, eight_ref, rows_ref, transfer_ref, base_ref, target_ref, out_ref):
    spread = spread_blocks(two_ref, four_ref, eight_ref, rows_ref, transfer_ref)
    finish(recv_ref, spread, base_ref, target_ref, out_ref)


def shape(*dims, dtype=BF16):
    return jax.ShapeDtypeStruct(dims, dtype)


def shards(
    density, panels, near_mask, source_basis, leaf_transfer, cluster_coupling,
    out_leaf, out_wide, out_target, coupling, target_basis,
):
    panels_here = LEAVES * LEAF_SIZE
    values = shape(RIGHT_SIDES, panels_here)
    packet_width = panels_here + 128
    merged_shape = shape(NA, LEAVES * ROWS, 128)
    coeff_work = pltpu.VMEM((LEAVES * RIGHT_SIDES, RANK), BF16)

    def swap(block, axis, distance):
        count = lax.axis_size(axis)
        return lax.ppermute(block, axis, [(i, i ^ distance) for i in range(count)])

    first = call(
        first_body, "first",
        [
            shape(PEERS, CHUNK + IDS, 128), shape(RIGHT_SIDES + PARTS * ROWS, packet_width),
            shape(2 * OUTS, dtype=jnp.int32),
        ],
        [pltpu.HBM] * 8,
        [
            pltpu.SMEM((OUTS,), jnp.int32),
            pltpu.SMEM((OUTS,), jnp.int32),
            pltpu.SMEM((OUTS,), jnp.int32),
            pltpu.VMEM((7, panels_here), F32),
            pltpu.VMEM((RIGHT_SIDES, panels_here), BF16),
            pltpu.VMEM((RANK, panels_here), BF16),
            pltpu.VMEM((LEAVES, RANK, RANK), BF16),
            pltpu.VMEM((OUTS, RANK, RANK), BF16),
            coeff_work,
            pltpu.VMEM((2 * PEERS * NA, 128), F32),
            pltpu.SMEM((NA * PEERS,), jnp.int32),
            pltpu.SemaphoreType.DMA((8,)),
        ],
        [VM, VM, SM],
    )
    first_merge = call(
        first_merge_body, "first_merge", [merged_shape, shape(NA, LEAVES * ROWS, 2 * 128)], [VM]
    )
    next_merge = call(merge_body, "merge", [merged_shape], [VM] * 2)
    nearby = call(near_body, "nearby", [shape(RIGHT_SIDES, panels_here, dtype=F32)], [VM] * 3)
    spreading = call(spread_body, "spread", [shape(LEAVES * ROWS, 128, dtype=F32)], [VM] * 5)

    def together(*arrays):
        return lax.optimization_barrier(arrays)

    def couple(value, send, packet, choice, kernel):
        columns = slice(panels_here, panels_here + RANK)
        arrived = lax.all_to_all(send, ("b", "y"), 0, 0, tiled=True)
        other = swap(packet, "c", 1)
        two = jnp.concatenate([packet[:RIGHT_SIDES, columns], other[:RIGHT_SIDES, columns]], axis=1)
        four = swap(two, "x", 1)
        if kernel is None:
            kernel = call(
                kernel_body, "kernel", [shape(panels_here, 2 * panels_here)], [VM, VM, SM],
                [pltpu.VMEM((8, panels_here), F32)],
            )(panels, other, near_mask)[0]
        base = nearby(value, other, kernel)[0]
        if choice is None:
            arrived, four, kernel = together(arrived, four, kernel)
        else:
            arrived, four, base = together(arrived, four, base)
        if choice is None:
            order = ORDER
            merged, choice = first_merge(arrived)
        else:
            order = LATER_ORDER
            merged = next_merge(arrived, choice)[0]
        merged, four = together(merged, four)
        received = lax.all_to_all(merged, "a", 0, 0, axis_index_groups=[order], tiled=True)
        eight = swap(jnp.concatenate([two, four], axis=1), "x", 3)
        return received, base, (two, four, eight, cluster_coupling, leaf_transfer), choice, kernel

    operands = (
        out_leaf, out_wide.reshape(OUTS), out_target, panels, density, source_basis, leaf_transfer, coupling
    )
    send, packet, place = first(*[pltpu.with_memory_space_constraint(array, pltpu.HBM) for array in operands])
    received, base, clusters, choice, kernel = couple(density, send, packet, None, None)
    first_pass, send, packet = call(
        middle_body, "middle", [values, shape(PEERS, CHUNK, 128), shape(RIGHT_SIDES, packet_width)],
        [VM] * 7 + [SM] + [VM] * 3, [coeff_work],
    )(received, *clusters[:4], base, target_basis, place, source_basis, leaf_transfer, coupling)

    received, base, clusters, choice, kernel = couple(first_pass, send, packet, choice, kernel)
    second_pass = call(last_body, "last", [values], [VM] * 8)(received, *clusters, base, target_basis)[0]
    return (first_pass, second_pass)


def solution(mesh):
    every = ("a", "b", "y", "x", "c")
    grid = Mesh(np.asarray(mesh.devices).reshape(NA, NB, NY, NX, NC), every)
    cols, rows = P(None, every), P(every)
    in_specs = (cols, cols, rows, cols, rows, rows, rows, rows, rows, rows, cols)
    return jax.shard_map(shards, mesh=grid, in_specs=in_specs, out_specs=(cols, cols), check_vma=False)
```
